512 devices in a mesh: dp: 64 (over x, z, y_lo), tensor: 8 (over y_hi, core).
Axes of the slice: x: 4, y: 8 (y_hi: 4, y_lo: 2; y = y_hi * 2 + y_lo), z: 8, core: 2. Of those that a mesh axis runs over, the one named last changes fastest.
Arguments:
- acts: bfloat16 [16384, 1024], P('dp'), may hold values from -8 to 8
- up_grad: bfloat16 [16384, 8192], P('dp', 'tensor'), may hold values from -8 to 8
Outputs:
- left_root: float32 [1024, 8192], P('dp', 'tensor')
- right_root: float32 [1024, 8192], P('dp', 'tensor')
- update: float32 [1024, 8192], P('dp', 'tensor')
The draws below stay inside these ranges and needn't reach their ends.
All inputs are finite; a program needn't handle non-finite values.
Results may differ from the reference program's by a relative error of at most 0.0011.
The reference program's roundings to bfloat16 on the way (of `grad_low`) count: a program that leaves them out, or rounds other values in their place, can miss the bound.
Values may be sent and summed in bfloat16 or wider, within the bound.
No kernel may reach another device: no remote copies, remote signals or barrier semaphores. Data moves between devices by JAX's collectives and lax.ppermute only.
A program may use at most 64 MiB of HBM per device.

```python
import math
import jax
import jax.numpy as jnp
from jax import lax

BLOCK = 1024
TOK_DEV = 256
NEWTON = 2
TOKENS = 16384
HIDDEN_WIN = 8192
N_TENSOR = 8


def token_weights(key, exponent):
    owners = TOKENS // TOK_DEV
    ranking = jax.random.permutation(jax.random.fold_in(key, 101), owners)
    weights = (ranking.astype(jnp.float32) + 1.0) ** (-exponent)
    factor = jax.random.normal(jax.random.fold_in(key, 102), (owners, TOK_DEV, 1), jnp.float32)
    return 0.45 * jnp.sqrt(weights)[:, None, None] * factor


def feature_scales(key, columns, rising):
    spread = jnp.exp(jax.random.uniform(key, (columns,), jnp.float32, math.log(0.3), math.log(3.0)))
    trend = rising ** (jnp.arange(columns, dtype=jnp.float32) / (columns - 1) - 0.5)
    return spread * trend


def draw_acts(key, part):
    exponent, rising = (0.5, 1.7320508)
    amplitude = token_weights(key, exponent)
    key = jax.random.fold_in(key, 1)
    owners = TOKENS // TOK_DEV
    block_shape = (owners, TOK_DEV, BLOCK)
    directions = jax.random.normal(jax.random.fold_in(key, 2), (owners, 1, BLOCK), jnp.float32)
    scales = feature_scales(jax.random.fold_in(key, 3), BLOCK, rising)
    values = amplitude * scales * directions
    noise_part = jax.random.normal(jax.random.fold_in(key, 4), block_shape, jnp.float32)
    return jnp.clip(values + noise_part, -8.0, 8.0).reshape(TOKENS, BLOCK).astype(jnp.bfloat16)


def draw_up_grad(key, part):
    exponent, rising = (0.5, 1.7320508)
    amplitude = token_weights(key, exponent)
    key = jax.random.fold_in(key, 2)
    owners = TOKENS // TOK_DEV
    block_shape = (owners, TOK_DEV, HIDDEN_WIN)
    directions = jax.random.normal(jax.random.fold_in(key, 2), (owners, 1, HIDDEN_WIN), jnp.float32)
    scales = feature_scales(jax.random.fold_in(key, 3), HIDDEN_WIN, rising)
    values = amplitude * scales * directions
    noise_part = jax.random.normal(jax.random.fold_in(key, 4), block_shape, jnp.float32)
    return jnp.clip(values + noise_part, -8.0, 8.0).reshape(TOKENS, HIDDEN_WIN).astype(jnp.bfloat16)


def setup_inputs(seed: int = 0) -> dict:
    streams_of = jax.random.split(jax.random.key(seed), 3)
    return {
        "acts": draw_acts(jax.random.fold_in(streams_of[2], 71), 0),
        "up_grad": draw_up_grad(jax.random.fold_in(streams_of[2], 71), 0),
    }


DAMPING = 1e-06

def newton(matrix):
    eye = jnp.eye(BLOCK, dtype=jnp.float32)
    root = eye
    for step in range(NEWTON):
        factor = (5.0 * eye - matrix) * 0.25
        root = jnp.dot(root, factor, precision=lax.Precision.HIGHEST)
        if step + 1 < NEWTON:
            for power in range(4):
                matrix = jnp.dot(matrix, factor, precision=lax.Precision.HIGHEST)
    return root

def reference(acts, up_grad):
    grad = jnp.dot(acts.T, up_grad, preferred_element_type=jnp.float32) / TOKENS
    grad_low = grad.astype(jnp.bfloat16)
    eye = jnp.eye(BLOCK, dtype=jnp.float32)
    lefts = []
    rights = []
    products = []
    for index in range(N_TENSOR):
        piece = lax.slice_in_dim(grad_low, index * BLOCK, (index + 1) * BLOCK, axis=1)
        piece_wide = piece.astype(jnp.float32)
        left_stat = jnp.dot(piece, piece.T, preferred_element_type=jnp.float32) + DAMPING * eye
        right_stat = jnp.dot(piece.T, piece, preferred_element_type=jnp.float32) + DAMPING * eye
        scale = jnp.sqrt(jnp.sum(left_stat * left_stat))
        left_root = newton(left_stat / scale)
        right_root = newton(right_stat / scale)
        inner = jnp.dot(left_root, piece_wide, precision=lax.Precision.HIGHEST)
        products.append(jnp.dot(inner, right_root, precision=lax.Precision.HIGHEST))
        lefts.append(left_root)
        rights.append(right_root)
    product = jnp.concatenate(products, axis=1)
    update = product / jnp.sqrt(jnp.mean(product * product) + 1e-06)
    return (jnp.concatenate(lefts, axis=1), jnp.concatenate(rights, axis=1), update)
```

```python
import jax
import jax.numpy as jnp
from jax import lax
from jax.experimental import pallas as pl
from jax.experimental.pallas import tpu as pltpu
from jax.sharding import Mesh, PartitionSpec as P

DAMPING = 1e-06
SIZES = (4, 8, 2, 4, 2)
NAMES = ("x", "z", "yl", "yh", "core")
DP = ("x", "z", "yl")
TENSOR = ("yh", "core")
PLANE = ("x", "yl")
F32 = jnp.float32
LOW = jnp.bfloat16


def times(vector, weight):
    rows = vector.shape[0]
    high = vector.astype(LOW)
    rest = (vector - high.astype(F32)).astype(LOW)
    both = jnp.dot(
        jnp.concatenate([high, rest], axis=0), weight, preferred_element_type=F32
    )
    return both[:rows] + both[rows:]


def roots_kernel(start_ref, tiles_ref, left_ref, right_ref, product_ref, total_ref, grad, flip):
    width = grad.shape[0]
    rows = left_ref.shape[0]
    n_tiles, high, wide = tiles_ref.shape
    start = pl.multiple_of(start_ref[0], rows)
    for index in range(n_tiles):
        col, row = index // 2, index % 2
        grad[row * high : (row + 1) * high, col * wide : (col + 1) * wide] = tiles_ref[index]
    for row in range(0, width, 256):
        for col in range(0, width, 256):
            flip[col : col + 256, row : row + 256] = grad[
                row : row + 256, col : col + 256
            ].T
    total = jnp.zeros((256, 256), F32)
    trace = jnp.zeros((256, width), F32)
    for row in range(0, width, 256):
        part = grad[row : row + 256, :]
        wide_part = part.astype(F32)
        trace += wide_part * wide_part
        for col in range(row, width, 256):
            stat = jnp.dot(part, flip[:, col : col + 256], preferred_element_type=F32)
            total += (1.0 if col == row else 2.0) * (stat * stat)
    square = jnp.sum(total) + 2.0 * DAMPING * jnp.sum(trace) + width * DAMPING * DAMPING
    inverse = lax.rsqrt(jnp.full((1, 1), square, F32))

    col_index = lax.broadcasted_iota(jnp.int32, (rows, width), 1)
    row_index = lax.broadcasted_iota(jnp.int32, (rows, width), 0)
    eye = (col_index == start + row_index).astype(F32)

    def finish(vector, outer):
        return (outer + DAMPING * vector) * inverse

    def stepped(vector, power):
        return (5.0 * vector - power) * 0.25

    def left_power(vector):
        return finish(vector, times(times(vector, grad[...]), flip[...]))

    first = jnp.dot(grad[pl.ds(start, rows), :], flip[...], preferred_element_type=F32)
    root = stepped(eye, finish(eye, first))
    vector = root
    for _ in range(4):
        vector = stepped(vector, left_power(vector))
    left = stepped(root, left_power(vector))
    left_ref[...] = left

    high_left = left.astype(LOW)
    rest_left = (left - high_left.astype(F32)).astype(LOW)
    both = jnp.dot(
        jnp.concatenate([high_left, rest_left, flip[pl.ds(start, rows), :]], axis=0),
        grad[...],
        preferred_element_type=F32,
    )
    product = both[:rows] + both[rows : 2 * rows]
    right = stepped(eye, finish(eye, both[2 * rows :]))

    def right_power(vector):
        return finish(vector, times(times(vector, flip[...]), grad[...]))

    product = stepped(product, right_power(product))
    root = jnp.concatenate([right, product], axis=0)
    vector = root
    for _ in range(4):
        vector = stepped(vector, right_power(vector))
    root = stepped(root, right_power(vector))
    right_ref[...] = root[:rows]
    product = root[rows:]
    product_ref[...] = product
    total_ref[...] = jnp.full(total_ref.shape, jnp.sum(product * product), F32)


def roots(start, tiles, rows, devices):
    width = 1024
    shape = jax.ShapeDtypeStruct((rows, width), F32)
    vmem = pl.BlockSpec(memory_space=pltpu.VMEM)
    return pl.pallas_call(
        roots_kernel,
        out_shape=(shape, shape, shape, jax.ShapeDtypeStruct((devices, 128), F32)),
        in_specs=[pl.BlockSpec(memory_space=pltpu.SMEM), vmem],
        out_specs=(vmem, vmem, vmem, vmem),
        scratch_shapes=[pltpu.VMEM((width, width), LOW), pltpu.VMEM((width, width), LOW)],
        compiler_params=pltpu.CompilerParams(vmem_limit_bytes=32 * 1024 * 1024),
    )(start, tiles)


def pack_kernel(core_ref, acts_ref, grad_ref, sent_ref):
    core = core_ref[0]
    for index in range(sent_ref.shape[0]):
        col, row = index // 2, index % 2
        begin = pl.multiple_of(row * 512 + core * 256, 256)
        sent_ref[index, :, :256] = acts_ref[:, pl.ds(begin, 256)]
        sent_ref[index, :, 256:] = grad_ref[:, col * 256 : (col + 1) * 256]


def pack(core, acts, up_grad, plane):
    vmem = pl.BlockSpec(memory_space=pltpu.VMEM)
    return pl.pallas_call(
        pack_kernel,
        out_shape=jax.ShapeDtypeStruct((plane, acts.shape[0], 512), LOW),
        in_specs=[pl.BlockSpec(memory_space=pltpu.SMEM), vmem, vmem],
        out_specs=vmem,
        compiler_params=pltpu.CompilerParams(vmem_limit_bytes=16 * 1024 * 1024),
    )(core.astype(jnp.int32).reshape(1), acts, up_grad)


def against(left, right):
    return lax.dot_general(left, right, (((0,), (0,)), ((), ())), preferred_element_type=F32)


def per_device(acts, up_grad):
    tokens, width = acts.shape
    owners = 64
    rows = width // owners
    plane = 8
    depth = 8
    core = lax.axis_index("core")
    sent = pack(core, acts, up_grad, plane)
    got = lax.all_to_all(sent, PLANE, 0, 0, tiled=True).reshape(plane * tokens, 512)
    mine, cols = got[:, :256], got[:, 256:]
    other = lax.ppermute(mine, "core", [(0, 1), (1, 0)])
    mine, other = against(mine, cols), against(other, cols)
    tile = jnp.where(
        core == 0, jnp.concatenate([mine, other]), jnp.concatenate([other, mine])
    ).reshape(depth, 64, 256)
    parts = lax.all_to_all(tile, "z", 0, 0, tiled=True)
    piece = (jnp.sum(parts, axis=0) / (tokens * owners)).astype(LOW)
    tile = lax.all_to_all(jnp.broadcast_to(piece[None], (depth, 64, 256)), "z", 0, 0, tiled=True)
    tile = tile.reshape(512, 256)
    tiles = lax.all_to_all(
        jnp.broadcast_to(tile[None], (plane, 512, 256)), PLANE, 0, 0, tiled=True
    )
    start = (lax.axis_index(DP) * rows).astype(jnp.int32).reshape(1)
    left, right, product, total = roots(start, tiles, rows, 512)
    totals = lax.all_to_all(total, DP + TENSOR, 0, 0, tiled=True)
    mean = jnp.sum(totals[:, 0]) / (width * width * 8)
    update = product * lax.rsqrt(mean + 1e-06)
    return (left, right, update)


def solution(mesh):
    fine = Mesh(mesh.devices.reshape(SIZES), NAMES)
    out = P(DP, TENSOR)
    return jax.shard_map(
        per_device,
        mesh=fine,
        in_specs=(P(DP, None), P(DP, TENSOR)),
        out_specs=(out, out, out),
        check_vma=False,
    )
```

```python
import jax
import jax.numpy as jnp
from jax import lax
from jax.experimental import pallas as pl
from jax.experimental.pallas import tpu as pltpu
from jax.sharding import Mesh, PartitionSpec as P

DAMPING = 1e-06
SIZES = (4, 4, 2, 2, 4, 2)
NAMES = ("x", "zh", "zl", "yl", "yh", "core")
DP = ("x", "zh", "zl", "yl")
TENSOR = ("yh", "core")
PLANE = ("x", "yl")
DEPTH = ("zh", "zl")
SPREAD = ("x", "zl", "yl", "yh", "core")
F32 = jnp.float32
LOW = jnp.bfloat16


def parts_of(vector):
    high = vector.astype(LOW)
    rest = (vector - high.astype(F32)).astype(LOW)
    return jnp.concatenate([high, rest], axis=0)


def times(vector, weight):
    rows = vector.shape[0]
    both = jnp.dot(parts_of(vector), weight, preferred_element_type=F32)
    return both[:rows] + both[rows:]


def roots_kernel(tiles_ref, left_ref, right_ref, product_ref, total_ref, grad, flip, keep):
    width = grad.shape[0]
    rows = left_ref.shape[0]
    n_tiles, high, wide = tiles_ref.shape
    groups = keep.shape[0] // rows
    first = (lax.axis_index("x") * 16 + lax.axis_index("zl") * 2 + lax.axis_index("yl")) * rows
    starts = [pl.multiple_of(first + group * (4 * rows), rows) for group in range(groups)]
    mine = pl.multiple_of(lax.axis_index("zh") * rows, rows)
    start = pl.multiple_of(first + lax.axis_index("zh") * (4 * rows), rows)
    for index in range(n_tiles):
        col, row = index // 2, index % 2
        grad[row * high : (row + 1) * high, col * wide : (col + 1) * wide] = tiles_ref[index]
    for row in range(0, width, 256):
        for col in range(0, width, 256):
            flip[col : col + 256, row : row + 256] = grad[
                row : row + 256, col : col + 256
            ].T
    total = jnp.zeros((256, 256), F32)
    trace = jnp.zeros((256, width), F32)
    for row in range(0, width, 256):
        part = grad[row : row + 256, :]
        wide_part = part.astype(F32)
        trace += wide_part * wide_part
        for col in range(row, width, 256):
            stat = jnp.dot(part, flip[:, col : col + 256], preferred_element_type=F32)
            total += (1.0 if col == row else 2.0) * (stat * stat)
    square = jnp.sum(total) + 2.0 * DAMPING * jnp.sum(trace) + width * DAMPING * DAMPING
    inverse = lax.rsqrt(jnp.full((1, 1), square, F32))

    col_index = lax.broadcasted_iota(jnp.int32, (rows, width), 1)
    row_index = lax.broadcasted_iota(jnp.int32, (rows, width), 0)

    def eye_of(begin):
        return (col_index == begin + row_index).astype(F32)

    def finish(vector, outer):
        return (outer + DAMPING * vector) * inverse

    def stepped(vector, power):
        return (5.0 * vector - power) * 0.25

    def left_power(vector):
        return finish(vector, times(times(vector, grad[...]), flip[...]))

    eyes = jnp.concatenate([eye_of(begin) for begin in starts], axis=0)
    chosen = jnp.concatenate([grad[pl.ds(begin, rows), :] for begin in starts], axis=0)
    outer = jnp.dot(chosen, flip[...], preferred_element_type=F32)
    root = stepped(eyes, finish(eyes, outer))
    vector = root
    for _ in range(4):
        vector = stepped(vector, left_power(vector))
    left = stepped(root, left_power(vector))
    keep[...] = left
    left_ref[...] = keep[pl.ds(mine, rows), :]

    eye = eye_of(start)
    count = groups * rows
    both = jnp.dot(
        jnp.concatenate([parts_of(left), flip[pl.ds(start, rows), :]], axis=0),
        grad[...],
        preferred_element_type=F32,
    )
    product = both[:count] + both[count : 2 * count]
    right = stepped(eye, finish(eye, both[2 * count :]))

    def right_power(vector):
        return finish(vector, times(times(vector, flip[...]), grad[...]))

    product = stepped(product, right_power(product))
    root = jnp.concatenate([right, product], axis=0)
    vector = root
    for _ in range(4):
        vector = stepped(vector, right_power(vector))
    root = stepped(root, right_power(vector))
    right_ref[...] = root[:rows]
    product = root[rows:]
    total_ref[...] = jnp.full(total_ref.shape, jnp.sum(product * product), F32)
    keep[...] = product
    product_ref[...] = keep[pl.ds(mine, rows), :]


def roots(tiles, rows, devices):
    width = 1024
    shape = jax.ShapeDtypeStruct((rows, width), F32)
    vmem = pl.BlockSpec(memory_space=pltpu.VMEM)
    return pl.pallas_call(
        roots_kernel,
        out_shape=(shape, shape, shape, jax.ShapeDtypeStruct((devices, 128), F32)),
        in_specs=[vmem],
        out_specs=(vmem, vmem, vmem, vmem),
        scratch_shapes=[
            pltpu.VMEM((width, width), LOW),
            pltpu.VMEM((width, width), LOW),
            pltpu.VMEM((4 * rows, width), F32),
        ],
        compiler_params=pltpu.CompilerParams(vmem_limit_bytes=32 * 1024 * 1024),
    )(tiles)


def pack_kernel(core_ref, acts_ref, grad_ref, sent_ref):
    core = core_ref[0]
    for index in range(sent_ref.shape[0]):
        col, row = index // 2, index % 2
        begin = pl.multiple_of(row * 512 + core * 256, 256)
        sent_ref[index, :, :256] = acts_ref[:, pl.ds(begin, 256)]
        sent_ref[index, :, 256:] = grad_ref[:, col * 256 : (col + 1) * 256]


def pack(core, acts, up_grad, plane):
    vmem = pl.BlockSpec(memory_space=pltpu.VMEM)
    return pl.pallas_call(
        pack_kernel,
        out_shape=jax.ShapeDtypeStruct((plane, acts.shape[0], 512), LOW),
        in_specs=[pl.BlockSpec(memory_space=pltpu.SMEM), vmem, vmem],
        out_specs=vmem,
        compiler_params=pltpu.CompilerParams(vmem_limit_bytes=16 * 1024 * 1024),
    )(core.astype(jnp.int32).reshape(1), acts, up_grad)


def against(left, right):
    return lax.dot_general(left, right, (((0,), (0,)), ((), ())), preferred_element_type=F32)


def per_device(acts, up_grad):
    tokens, width = acts.shape
    owners = 64
    rows = width // owners
    plane = 8
    depth = 8
    core = lax.axis_index("core")
    sent = pack(core, acts, up_grad, plane)
    got = lax.all_to_all(sent, PLANE, 0, 0, tiled=True).reshape(plane * tokens, 512)
    mine, cols = got[:, :256], got[:, 256:]
    other = lax.ppermute(mine, "core", [(0, 1), (1, 0)])
    mine, other = against(mine, cols), against(other, cols)
    tile = jnp.where(
        core == 0, jnp.concatenate([mine, other]), jnp.concatenate([other, mine])
    ).reshape(depth, 64, 256)
    parts = lax.all_to_all(tile, DEPTH, 0, 0, tiled=True)
    piece = (jnp.sum(parts, axis=0) / (tokens * owners)).astype(LOW)
    tile = lax.all_to_all(jnp.broadcast_to(piece[None], (depth, 64, 256)), DEPTH, 0, 0, tiled=True)
    tile = tile.reshape(512, 256)
    tiles = lax.all_to_all(
        jnp.broadcast_to(tile[None], (plane, 512, 256)), PLANE, 0, 0, tiled=True
    )
    left, right, product, total = roots(tiles, rows, 128)
    totals = lax.all_to_all(total, SPREAD, 0, 0, tiled=True)
    mean = jnp.sum(totals[:, 0]) / (width * width * 8)
    update = product * lax.rsqrt(mean + 1e-06)
    return (left, right, update)


def solution(mesh):
    fine = Mesh(mesh.devices.reshape(SIZES), NAMES)
    out = P(DP, TENSOR)
    return jax.shard_map(
        per_device,
        mesh=fine,
        in_specs=(P(DP, None), P(DP, TENSOR)),
        out_specs=(out, out, out),
        check_vma=False,
    )
```

```python
import jax
import jax.numpy as jnp
from jax import lax
from jax.experimental import pallas as pl
from jax.experimental.pallas import tpu as pltpu
from jax.sharding import Mesh, PartitionSpec as P

DAMPING = 1e-06
SIZES = (4, 4, 2, 2, 4, 2)
NAMES = ("x", "zh", "zl", "yl", "yh", "core")
DP = ("x", "zh", "zl", "yl")
TENSOR = ("yh", "core")
PLANE = ("x", "yl")
DEPTH = ("zh", "zl")
SPREAD = ("x", "zl", "yl", "yh", "core")
F32 = jnp.float32
LOW = jnp.bfloat16
ACROSS = (((1,), (1,)), ((), ()))


def parts_of(vector):
    high = vector.astype(LOW)
    rest = (vector - high.astype(F32)).astype(LOW)
    return jnp.concatenate([high, rest], axis=0)


def times(vector, weight):
    rows = vector.shape[0]
    both = jnp.dot(parts_of(vector), weight, preferred_element_type=F32)
    return both[:rows] + both[rows:]


def roots_kernel(
    tiles_ref, left_ref, right_ref, product_ref, total_ref, grad, stat, rest, turned, keep
):
    width = grad.shape[0]
    rows = left_ref.shape[0]
    n_tiles, high, wide = tiles_ref.shape
    groups = keep.shape[0] // rows
    count = groups * rows
    first = (lax.axis_index("x") * 16 + lax.axis_index("zl") * 2 + lax.axis_index("yl")) * rows
    starts = [pl.multiple_of(first + group * (4 * rows), rows) for group in range(groups)]
    mine = pl.multiple_of(lax.axis_index("zh") * rows, rows)
    start = pl.multiple_of(first + lax.axis_index("zh") * (4 * rows), rows)
    for index in range(n_tiles):
        col, row = index // 2, index % 2
        grad[row * high : (row + 1) * high, col * wide : (col + 1) * wide] = tiles_ref[index]

    side = 256
    on_diagonal = lax.broadcasted_iota(jnp.int32, (side, side), 0) == lax.broadcasted_iota(
        jnp.int32, (side, side), 1
    )
    squares = crossed = squared = jnp.zeros((side, side), F32)
    diagonal, rounded = [], []
    for row in range(0, width, side):
        part = grad[row : row + side, :]
        for col in range(row, width, side):
            tile = lax.dot_general(
                part, grad[col : col + side, :], ACROSS, preferred_element_type=F32
            )
            tile_low = tile.astype(LOW)
            back = tile_low.astype(F32)
            tile_rest = (tile - back).astype(LOW)
            stat[row : row + side, col : col + side] = tile_low
            rest[row : row + side, col : col + side] = tile_rest
            if col > row:
                stat[col : col + side, row : row + side] = tile_low.T
                rest[col : col + side, row : row + side] = tile_rest.T
                squares += 2.0 * (tile * tile)
                crossed += tile * back
                squared += back * back
            else:
                outside = jnp.where(on_diagonal, 0.0, back)
                damped = jnp.where(on_diagonal, tile + DAMPING, tile)
                squares += damped * damped
                crossed += 0.5 * (tile * outside)
                squared += 0.5 * (outside * outside)
                diagonal.append(jnp.sum(jnp.where(on_diagonal, tile, 0.0), axis=0, keepdims=True))
                rounded.append(jnp.sum(jnp.where(on_diagonal, back, 0.0), axis=0, keepdims=True))
    inverse = lax.rsqrt(jnp.full((1, 1), jnp.sum(squares), F32))
    above = jnp.full((1, 1), jnp.sum(crossed), F32)
    below = jnp.full((1, 1), jnp.sum(squared), F32)
    gain = jnp.where(below > 0.0, above / jnp.where(below > 0.0, below, 1.0), 1.0)
    delta = DAMPING * inverse
    tau = 1.25 - 0.25 * delta
    own = tau - (0.25 * inverse) * (
        jnp.concatenate(diagonal, axis=1) - gain * jnp.concatenate(rounded, axis=1)
    )
    shared = 0.25 * inverse * gain

    def stepped(vector):
        return own * vector - shared * times(vector, stat[...])

    col_index = lax.broadcasted_iota(jnp.int32, (rows, width), 1)
    row_index = lax.broadcasted_iota(jnp.int32, (rows, width), 0)

    def eye_of(begin):
        return (col_index == begin + row_index).astype(F32)

    def chosen(begin):
        return stat[pl.ds(begin, rows), :].astype(F32) + rest[pl.ds(begin, rows), :].astype(F32)

    eyes = jnp.concatenate([eye_of(begin) for begin in starts], axis=0)
    power = jnp.concatenate([chosen(begin) for begin in starts], axis=0)
    power = (power + DAMPING * eyes) * inverse
    block = pl.multiple_of(start // 128 * 128, 128)
    turned[...] = grad[:, pl.ds(block, 128)].T
    column = turned[pl.ds(pl.multiple_of(start - block, rows), rows), :].astype(F32)
    small = 0.0625 * delta
    square = tau * tau
    factors = [small * (square * tau), small * square, small * tau, small]
    vector = jnp.concatenate([power, column], axis=0)
    inner = (0.3125 - small * (square * square)) * column
    for factor in factors:
        vector = stepped(vector)
        inner -= factor * vector[count:]
    vector = stepped(vector)
    inner += 0.25 * vector[count:]
    left = 1.5625 * eyes - (0.3125 * power + 0.25 * vector[:count])
    keep[...] = left
    left_ref[...] = keep[pl.ds(mine, rows), :]

    power = times(left, stat[...]) + jnp.dot(
        left.astype(LOW), rest[...], preferred_element_type=F32
    )
    power = (power + DAMPING * left) * inverse
    vector = power
    for _ in range(5):
        vector = stepped(vector)
    twice = 1.5625 * left - (0.3125 * power + 0.25 * vector)
    out = times(jnp.concatenate([inner, twice], axis=0), grad[...])
    base = 1.5625 - delta * (0.3125 + 0.25 * (square * square * tau))
    right_ref[...] = base * eye_of(start) - inverse * out[:rows]
    product = out[rows:]
    total_ref[...] = jnp.full(total_ref.shape, jnp.sum(product * product), F32)
    keep[...] = product
    product_ref[...] = keep[pl.ds(mine, rows), :]


def roots(tiles, rows, devices):
    width = 1024
    shape = jax.ShapeDtypeStruct((rows, width), F32)
    vmem = pl.BlockSpec(memory_space=pltpu.VMEM)
    return pl.pallas_call(
        roots_kernel,
        out_shape=(shape, shape, shape, jax.ShapeDtypeStruct((devices, 128), F32)),
        in_specs=[vmem],
        out_specs=(vmem, vmem, vmem, vmem),
        scratch_shapes=[
            pltpu.VMEM((width, width), LOW),
            pltpu.VMEM((width, width), LOW),
            pltpu.VMEM((width, width), LOW),
            pltpu.VMEM((128, width), LOW),
            pltpu.VMEM((4 * rows, width), F32),
        ],
        compiler_params=pltpu.CompilerParams(vmem_limit_bytes=32 * 1024 * 1024),
    )(tiles)


def pack_kernel(core_ref, acts_ref, grad_ref, sent_ref):
    core = core_ref[0]
    for index in range(sent_ref.shape[0]):
        col, row = index // 2, index % 2
        begin = pl.multiple_of(row * 512 + core * 256, 256)
        sent_ref[index, :, :256] = acts_ref[:, pl.ds(begin, 256)]
        sent_ref[index, :, 256:] = grad_ref[:, col * 256 : (col + 1) * 256]


def pack(core, acts, up_grad, plane):
    vmem = pl.BlockSpec(memory_space=pltpu.VMEM)
    return pl.pallas_call(
        pack_kernel,
        out_shape=jax.ShapeDtypeStruct((plane, acts.shape[0], 512), LOW),
        in_specs=[pl.BlockSpec(memory_space=pltpu.SMEM), vmem, vmem],
        out_specs=vmem,
        compiler_params=pltpu.CompilerParams(vmem_limit_bytes=16 * 1024 * 1024),
    )(core.astype(jnp.int32).reshape(1), acts, up_grad)


def against(left, right):
    return lax.dot_general(left, right, (((0,), (0,)), ((), ())), preferred_element_type=F32)


def per_device(acts, up_grad):
    tokens, width = acts.shape
    owners = 64
    rows = width // owners
    plane = 8
    depth = 8
    core = lax.axis_index("core")
    sent = pack(core, acts, up_grad, plane)
    got = lax.all_to_all(sent, PLANE, 0, 0, tiled=True).reshape(plane * tokens, 512)
    mine, cols = got[:, :256], got[:, 256:]
    other = lax.ppermute(mine, "core", [(0, 1), (1, 0)])
    mine, other = against(mine, cols), against(other, cols)
    tile = jnp.where(
        core == 0, jnp.concatenate([mine, other]), jnp.concatenate([other, mine])
    ).reshape(depth, 64, 256)
    parts = lax.all_to_all(tile, DEPTH, 0, 0, tiled=True)
    piece = (jnp.sum(parts, axis=0) / (tokens * owners)).astype(LOW)
    tile = lax.all_to_all(jnp.broadcast_to(piece[None], (depth, 64, 256)), DEPTH, 0, 0, tiled=True)
    tile = tile.reshape(512, 256)
    tiles = lax.all_to_all(
        jnp.broadcast_to(tile[None], (plane, 512, 256)), PLANE, 0, 0, tiled=True
    )
    left, right, product, total = roots(tiles, rows, 128)
    totals = lax.all_to_all(total, SPREAD, 0, 0, tiled=True)
    mean = jnp.sum(totals[:, 0]) / (width * width * 8)
    update = product * lax.rsqrt(mean + 1e-06)
    return (left, right, update)


def solution(mesh):
    fine = Mesh(mesh.devices.reshape(SIZES), NAMES)
    out = P(DP, TENSOR)
    return jax.shard_map(
        per_device,
        mesh=fine,
        in_specs=(P(DP, None), P(DP, TENSOR)),
        out_specs=(out, out, out),
        check_vma=False,
    )
```

```python
import jax
import jax.numpy as jnp
from jax import lax
from jax.experimental import pallas as pl
from jax.experimental.pallas import tpu as pltpu
from jax.sharding import Mesh, PartitionSpec as P

DAMPING = 1e-06
SIZES = (4, 4, 2, 2, 4, 2)
NAMES = ("x", "zh", "zl", "yl", "yh", "core")
DP = ("x", "zh", "zl", "yl")
TENSOR = ("yh", "core")
PLANE = ("x", "yl")
DEPTH = ("zh", "zl")
SPREAD = ("x", "zl", "yl", "yh", "core")
F32 = jnp.float32
LOW = jnp.bfloat16
ACROSS = (((1,), (1,)), ((), ()))


def parts_of(vector):
    high = vector.astype(LOW)
    rest = (vector - high.astype(F32)).astype(LOW)
    return jnp.concatenate([high, rest], axis=0)


def times(vector, weight):
    rows = vector.shape[0]
    both = jnp.dot(parts_of(vector), weight, preferred_element_type=F32)
    return both[:rows] + both[rows:]


def roots_kernel(
    tiles_ref, left_ref, right_ref, product_ref, total_ref, grad, stat, rest, turned, keep
):
    width = grad.shape[0]
    rows = left_ref.shape[0]
    n_tiles, high, wide = tiles_ref.shape
    groups = keep.shape[0] // rows
    count = groups * rows
    first = (lax.axis_index("x") * 16 + lax.axis_index("zl") * 2 + lax.axis_index("yl")) * rows
    starts = [pl.multiple_of(first + group * (4 * rows), rows) for group in range(groups)]
    mine = pl.multiple_of(lax.axis_index("zh") * rows, rows)
    start = pl.multiple_of(first + lax.axis_index("zh") * (4 * rows), rows)
    for index in range(n_tiles):
        col, row = index // 2, index % 2
        grad[row * high : (row + 1) * high, col * wide : (col + 1) * wide] = tiles_ref[index]

    side = 256
    on_diagonal = lax.broadcasted_iota(jnp.int32, (side, side), 0) == lax.broadcasted_iota(
        jnp.int32, (side, side), 1
    )
    squares = crossed = squared = jnp.zeros((side, side), F32)
    diagonal, rounded = [], []
    for row in range(0, width, side):
        part = grad[row : row + side, :]
        for col in range(row, width, side):
            tile = lax.dot_general(
                part, grad[col : col + side, :], ACROSS, preferred_element_type=F32
            )
            tile_low = tile.astype(LOW)
            back = tile_low.astype(F32)
            tile_rest = (tile - back).astype(LOW)
            stat[row : row + side, col : col + side] = tile_low
            rest[row : row + side, col : col + side] = tile_rest
            if col > row:
                stat[col : col + side, row : row + side] = tile_low.T
                rest[col : col + side, row : row + side] = tile_rest.T
                squares += 2.0 * (tile * tile)
                crossed += tile * back
                squared += back * back
            else:
                outside = jnp.where(on_diagonal, 0.0, back)
                damped = jnp.where(on_diagonal, tile + DAMPING, tile)
                squares += damped * damped
                crossed += 0.5 * (tile * outside)
                squared += 0.5 * (outside * outside)
                diagonal.append(jnp.sum(jnp.where(on_diagonal, tile, 0.0), axis=0, keepdims=True))
                rounded.append(jnp.sum(jnp.where(on_diagonal, back, 0.0), axis=0, keepdims=True))
    inverse = lax.rsqrt(jnp.full((1, 1), jnp.sum(squares), F32))
    above = jnp.full((1, 1), jnp.sum(crossed), F32)
    below = jnp.full((1, 1), jnp.sum(squared), F32)
    gain = jnp.where(below > 0.0, above / jnp.where(below > 0.0, below, 1.0), 1.0)
    delta = DAMPING * inverse
    tau = 1.25 - 0.25 * delta
    own = tau - (0.25 * inverse) * (
        jnp.concatenate(diagonal, axis=1) - gain * jnp.concatenate(rounded, axis=1)
    )
    shared = 0.25 * inverse * gain

    def stepped(vector):
        return own * vector - shared * times(vector, stat[...])

    col_index = lax.broadcasted_iota(jnp.int32, (rows, width), 1)
    row_index = lax.broadcasted_iota(jnp.int32, (rows, width), 0)

    def eye_of(begin):
        return (col_index == begin + row_index).astype(F32)

    def chosen(begin):
        return stat[pl.ds(begin, rows), :].astype(F32) + rest[pl.ds(begin, rows), :].astype(F32)

    eyes = jnp.concatenate([eye_of(begin) for begin in starts], axis=0)
    power = jnp.concatenate([chosen(begin) for begin in starts], axis=0)
    power = (power + DAMPING * eyes) * inverse
    block = pl.multiple_of(start // 128 * 128, 128)
    turned[...] = grad[:, pl.ds(block, 128)].T
    column = turned[pl.ds(pl.multiple_of(start - block, rows), rows), :].astype(F32)
    small = 0.0625 * delta
    square = tau * tau
    factors = [small * (square * tau), small * square, small * tau, small]
    vector = jnp.concatenate([power, column], axis=0)
    inner = (0.3125 - small * (square * square)) * column
    for factor in factors:
        vector = stepped(vector)
        inner -= factor * vector[count:]
    vector = stepped(vector)
    inner += 0.25 * vector[count:]
    left = 1.5625 * eyes - (0.3125 * power + 0.25 * vector[:count])
    keep[...] = left
    left_ref[...] = keep[pl.ds(mine, rows), :]

    power = times(left, stat[...]) + jnp.dot(
        left.astype(LOW), rest[...], preferred_element_type=F32
    )
    power = (power + DAMPING * left) * inverse
    vector = power
    for _ in range(5):
        vector = stepped(vector)
    twice = 1.5625 * left - (0.3125 * power + 0.25 * vector)
    out = times(jnp.concatenate([inner, twice], axis=0), grad[...])
    base = 1.5625 - delta * (0.3125 + 0.25 * (square * square * tau))
    right_ref[...] = base * eye_of(start) - inverse * out[:rows]
    product = out[rows:]
    total_ref[...] = jnp.full(total_ref.shape, jnp.sum(product * product), F32)
    keep[...] = product
    product_ref[...] = keep[pl.ds(mine, rows), :]


def roots(tiles, rows, devices):
    width = 1024
    shape = jax.ShapeDtypeStruct((rows, width), F32)
    vmem = pl.BlockSpec(memory_space=pltpu.VMEM)
    return pl.pallas_call(
        roots_kernel,
        out_shape=(shape, shape, shape, jax.ShapeDtypeStruct((devices, 128), F32)),
        in_specs=[vmem],
        out_specs=(vmem, vmem, vmem, vmem),
        scratch_shapes=[
            pltpu.VMEM((width, width), LOW),
            pltpu.VMEM((width, width), LOW),
            pltpu.VMEM((width, width), LOW),
            pltpu.VMEM((128, width), LOW),
            pltpu.VMEM((4 * rows, width), F32),
        ],
        compiler_params=pltpu.CompilerParams(vmem_limit_bytes=32 * 1024 * 1024),
    )(tiles)


def against(left, right):
    return lax.dot_general(left, right, (((0,), (0,)), ((), ())), preferred_element_type=F32)


def per_device(acts, up_grad):
    tokens, width = acts.shape
    owners = 64
    rows = width // owners
    plane = 8
    depth = 8
    core = lax.axis_index("core")
    halves = [
        lax.dynamic_slice_in_dim(acts, row * 512 + core * 256, 256, 1) for row in range(2)
    ]
    sent = jnp.stack(
        [
            jnp.concatenate([halves[i % 2], up_grad[:, i // 2 * 256 : i // 2 * 256 + 256]], axis=1)
            for i in range(plane)
        ]
    )
    got = lax.all_to_all(sent, PLANE, 0, 0, tiled=True).reshape(plane * tokens, 512)
    mine, cols = got[:, :256], got[:, 256:]
    other = lax.ppermute(mine, "core", [(0, 1), (1, 0)])
    mine, other = against(mine, cols), against(other, cols)
    tile = jnp.where(
        core == 0, jnp.concatenate([mine, other]), jnp.concatenate([other, mine])
    ).reshape(depth, 64, 256)
    parts = lax.all_to_all(tile, DEPTH, 0, 0, tiled=True)
    piece = (jnp.sum(parts, axis=0) / (tokens * owners)).astype(LOW)
    tile = lax.all_to_all(jnp.broadcast_to(piece[None], (depth, 64, 256)), DEPTH, 0, 0, tiled=True)
    tile = tile.reshape(512, 256)
    tiles = lax.all_to_all(
        jnp.broadcast_to(tile[None], (plane, 512, 256)), PLANE, 0, 0, tiled=True
    )
    left, right, product, total = roots(tiles, rows, 128)
    totals = lax.all_to_all(total, SPREAD, 0, 0, tiled=True)
    mean = jnp.sum(totals[:, 0]) / (width * width * 8)
    update = product * lax.rsqrt(mean + 1e-06)
    return (left, right, update)


def solution(mesh):
    fine = Mesh(mesh.devices.reshape(SIZES), NAMES)
    out = P(DP, TENSOR)
    return jax.shard_map(
        per_device,
        mesh=fine,
        in_specs=(P(DP, None), P(DP, TENSOR)),
        out_specs=(out, out, out),
        check_vma=False,
    )
```

```python
import jax
import jax.numpy as jnp
from jax import lax
from jax.experimental import pallas as pl
from jax.experimental.pallas import tpu as pltpu
from jax.sharding import Mesh, PartitionSpec as P

DAMPING = 1e-06
SIZES = (4, 4, 2, 2, 4, 2)
NAMES = ("x", "zh", "zl", "yl", "yh", "core")
DP = ("x", "zh", "zl", "yl")
TENSOR = ("yh", "core")
PLANE = ("x", "yl")
DEPTH = ("zh", "zl")
SPREAD = ("x", "zl", "yl", "yh", "core")
F32 = jnp.float32
LOW = jnp.bfloat16
ACROSS = (((1,), (1,)), ((), ()))


def parts_of(vector):
    high = vector.astype(LOW)
    rest = (vector - high.astype(F32)).astype(LOW)
    return jnp.concatenate([high, rest], axis=0)


def times(vector, weight):
    rows = vector.shape[0]
    both = jnp.dot(parts_of(vector), weight, preferred_element_type=F32)
    return both[:rows] + both[rows:]


def roots_kernel(
    tiles_ref, left_ref, right_ref, product_ref, total_ref, grad, stat, rest, turned, keep
):
    width = grad.shape[0]
    rows = left_ref.shape[0]
    n_tiles, high, wide = tiles_ref.shape
    groups = keep.shape[0] // rows
    count = groups * rows
    first = (lax.axis_index("x") * 16 + lax.axis_index("zl") * 2 + lax.axis_index("yl")) * rows
    starts = [pl.multiple_of(first + group * (4 * rows), rows) for group in range(groups)]
    mine = pl.multiple_of(lax.axis_index("zh") * rows, rows)
    start = pl.multiple_of(first + lax.axis_index("zh") * (4 * rows), rows)
    for index in range(n_tiles):
        col, row = index // 2, index % 2
        grad[row * high : (row + 1) * high, col * wide : (col + 1) * wide] = tiles_ref[index]

    side = 256
    on_diagonal = lax.broadcasted_iota(jnp.int32, (side, side), 0) == lax.broadcasted_iota(
        jnp.int32, (side, side), 1
    )
    squares = crossed = squared = jnp.zeros((side, side), F32)
    diagonal, rounded = [], []
    for row in range(0, width, side):
        part = grad[row : row + side, :]
        for col in range(row, width, side):
            tile = lax.dot_general(
                part, grad[col : col + side, :], ACROSS, preferred_element_type=F32
            )
            tile_low = tile.astype(LOW)
            back = tile_low.astype(F32)
            tile_rest = (tile - back).astype(LOW)
            stat[row : row + side, col : col + side] = tile_low
            rest[row : row + side, col : col + side] = tile_rest
            if col > row:
                stat[col : col + side, row : row + side] = tile_low.T
                rest[col : col + side, row : row + side] = tile_rest.T
                squares += 2.0 * (tile * tile)
                crossed += tile * back
                squared += back * back
            else:
                outside = jnp.where(on_diagonal, 0.0, back)
                damped = jnp.where(on_diagonal, tile + DAMPING, tile)
                squares += damped * damped
                crossed += 0.5 * (tile * outside)
                squared += 0.5 * (outside * outside)
                diagonal.append(jnp.sum(jnp.where(on_diagonal, tile, 0.0), axis=0, keepdims=True))
                rounded.append(jnp.sum(jnp.where(on_diagonal, back, 0.0), axis=0, keepdims=True))
    inverse = lax.rsqrt(jnp.full((1, 1), jnp.sum(squares), F32))
    above = jnp.full((1, 1), jnp.sum(crossed), F32)
    below = jnp.full((1, 1), jnp.sum(squared), F32)
    gain = jnp.where(below > 0.0, above / jnp.where(below > 0.0, below, 1.0), 1.0)
    delta = DAMPING * inverse
    tau = 1.25 - 0.25 * delta
    own = tau - (0.25 * inverse) * (
        jnp.concatenate(diagonal, axis=1) - gain * jnp.concatenate(rounded, axis=1)
    )
    shared = 0.25 * inverse * gain

    def stepped(vector):
        return own * vector - shared * times(vector, stat[...])

    col_index = lax.broadcasted_iota(jnp.int32, (rows, width), 1)
    row_index = lax.broadcasted_iota(jnp.int32, (rows, width), 0)

    def eye_of(begin):
        return (col_index == begin + row_index).astype(F32)

    def chosen(begin):
        return stat[pl.ds(begin, rows), :].astype(F32) + rest[pl.ds(begin, rows), :].astype(F32)

    eyes = jnp.concatenate([eye_of(begin) for begin in starts], axis=0)
    power = jnp.concatenate([chosen(begin) for begin in starts], axis=0)
    power = (power + DAMPING * eyes) * inverse
    block = pl.multiple_of(start // 128 * 128, 128)
    turned[...] = grad[:, pl.ds(block, 128)].T
    column = turned[pl.ds(pl.multiple_of(start - block, rows), rows), :].astype(F32)
    small = 0.0625 * delta
    square = tau * tau
    factors = [small * (square * tau), small * square, small * tau, small]
    vector = jnp.concatenate([power, column], axis=0)
    inner = (0.3125 - small * (square * square)) * column
    for factor in factors:
        vector = stepped(vector)
        inner -= factor * vector[count:]
    vector = stepped(vector)
    inner += 0.25 * vector[count:]
    left = 1.5625 * eyes - (0.3125 * power + 0.25 * vector[:count])
    keep[...] = left
    left_ref[...] = keep[pl.ds(mine, rows), :]

    power = times(left, stat[...]) + jnp.dot(
        left.astype(LOW), rest[...], preferred_element_type=F32
    )
    power = (power + DAMPING * left) * inverse
    vector = power
    for _ in range(5):
        vector = stepped(vector)
    twice = 1.5625 * left - (0.3125 * power + 0.25 * vector)
    out = times(jnp.concatenate([inner, twice], axis=0), grad[...])
    base = 1.5625 - delta * (0.3125 + 0.25 * (square * square * tau))
    right_ref[...] = base * eye_of(start) - inverse * out[:rows]
    product = out[rows:]
    total_ref[...] = jnp.full(total_ref.shape, jnp.sum(product * product), F32)
    keep[...] = product
    product_ref[...] = keep[pl.ds(mine, rows), :]


def roots(tiles, rows, devices):
    width = 1024
    shape = jax.ShapeDtypeStruct((rows, width), F32)
    vmem = pl.BlockSpec(memory_space=pltpu.VMEM)
    return pl.pallas_call(
        roots_kernel,
        out_shape=(shape, shape, shape, jax.ShapeDtypeStruct((devices, 128), F32)),
        in_specs=[vmem],
        out_specs=(vmem, vmem, vmem, vmem),
        scratch_shapes=[
            pltpu.VMEM((width, width), LOW),
            pltpu.VMEM((width, width), LOW),
            pltpu.VMEM((width, width), LOW),
            pltpu.VMEM((128, width), LOW),
            pltpu.VMEM((4 * rows, width), F32),
        ],
        compiler_params=pltpu.CompilerParams(vmem_limit_bytes=32 * 1024 * 1024),
    )(tiles)


def cut_kernel(got_ref, mine_ref):
    mine_ref[...] = got_ref[:, : mine_ref.shape[1]]


def cut(got, columns):
    vmem = pl.BlockSpec(memory_space=pltpu.VMEM)
    return pl.pallas_call(
        cut_kernel,
        out_shape=jax.ShapeDtypeStruct((got.shape[0], columns), LOW),
        in_specs=[vmem],
        out_specs=vmem,
        compiler_params=pltpu.CompilerParams(vmem_limit_bytes=16 * 1024 * 1024),
    )(got)


def against(left, right):
    return lax.dot_general(left, right, (((0,), (0,)), ((), ())), preferred_element_type=F32)


def join_kernel(got_ref, other_ref, mine_ref, tile_ref):
    core = lax.axis_index("core")
    half = mine_ref.shape[0]
    tile_ref[pl.ds(pl.multiple_of(core * half, half), half), :] = mine_ref[...]
    tile_ref[pl.ds(pl.multiple_of((1 - core) * half, half), half), :] = against(
        other_ref[...], got_ref[:, half:]
    )


def join(got, other, mine):
    vmem = pl.BlockSpec(memory_space=pltpu.VMEM)
    rows, columns = mine.shape
    return pl.pallas_call(
        join_kernel,
        out_shape=jax.ShapeDtypeStruct((2 * rows, columns), F32),
        in_specs=[vmem, vmem, vmem],
        out_specs=vmem,
        compiler_params=pltpu.CompilerParams(vmem_limit_bytes=16 * 1024 * 1024),
    )(got, other, mine)


def per_device(acts, up_grad):
    tokens, width = acts.shape
    owners = 64
    rows = width // owners
    plane = 8
    depth = 8
    core = lax.axis_index("core")
    halves = [
        lax.dynamic_slice_in_dim(acts, row * 512 + core * 256, 256, 1) for row in range(2)
    ]
    sent = jnp.stack(
        [
            jnp.concatenate([halves[i % 2], up_grad[:, i // 2 * 256 : i // 2 * 256 + 256]], axis=1)
            for i in range(plane)
        ]
    )
    got = lax.all_to_all(sent, PLANE, 0, 0, tiled=True).reshape(plane * tokens, 512)
    other = lax.ppermute(cut(got, 256), "core", [(0, 1), (1, 0)])
    tile = join(got, other, against(got[:, :256], got[:, 256:])).reshape(depth, 64, 256)
    parts = lax.all_to_all(tile, DEPTH, 0, 0, tiled=True)
    piece = (jnp.sum(parts, axis=0) / (tokens * owners)).astype(LOW)
    tile = lax.all_to_all(jnp.broadcast_to(piece[None], (depth, 64, 256)), DEPTH, 0, 0, tiled=True)
    tile = tile.reshape(512, 256)
    tiles = lax.all_to_all(
        jnp.broadcast_to(tile[None], (plane, 512, 256)), PLANE, 0, 0, tiled=True
    )
    left, right, product, total = roots(tiles, rows, 128)
    totals = lax.all_to_all(total, SPREAD, 0, 0, tiled=True)
    mean = jnp.sum(totals, axis=0, keepdims=True)[:, :1] / (width * width * 8)
    update = product * lax.rsqrt(mean + 1e-06)
    return (left, right, update)


def solution(mesh):
    fine = Mesh(mesh.devices.reshape(SIZES), NAMES)
    out = P(DP, TENSOR)
    return jax.shard_map(
        per_device,
        mesh=fine,
        in_specs=(P(DP, None), P(DP, TENSOR)),
        out_specs=(out, out, out),
        check_vma=False,
    )
```

```python
import jax
import jax.numpy as jnp
from jax import lax
from jax.experimental import pallas as pl
from jax.experimental.pallas import tpu as pltpu
from jax.sharding import Mesh, PartitionSpec as P

DAMPING = 1e-06
SIZES = (4, 4, 2, 2, 4, 2)
NAMES = ("x", "zh", "zl", "yl", "yh", "core")
DP = ("x", "zh", "zl", "yl")
TENSOR = ("yh", "core")
PLANE = ("x", "yl")
DEPTH = ("zh", "zl")
SPREAD = ("x", "zl", "yl", "yh", "core")
F32 = jnp.float32
LOW = jnp.bfloat16
ACROSS = (((1,), (1,)), ((), ()))


def parts_of(vector):
    high = vector.astype(LOW)
    rest = (vector - high.astype(F32)).astype(LOW)
    return jnp.concatenate([high, rest], axis=0)


def times(vector, weight):
    rows = vector.shape[0]
    both = jnp.dot(parts_of(vector), weight, preferred_element_type=F32)
    return both[:rows] + both[rows:]


def roots_kernel(mine_ref, other_ref, rows_ref, total_ref, grad, stat, rest, turned, keep):
    width = grad.shape[0]
    rows = rows_ref.shape[0] // 3
    n_tiles, high, wide = mine_ref.shape
    groups = keep.shape[0] // rows
    count = groups * rows
    core = lax.axis_index("core")
    first = (lax.axis_index("x") * 16 + core * 2 + lax.axis_index("yl")) * rows
    starts = [pl.multiple_of(first + group * (4 * rows), rows) for group in range(groups)]
    mine = pl.multiple_of(lax.axis_index("zh") * rows, rows)
    start = pl.multiple_of(first + lax.axis_index("zh") * (4 * rows), rows)
    for index in range(n_tiles):
        col, row = index // 2, index % 2
        here = pl.multiple_of((2 * row + core) * high, high)
        there = pl.multiple_of((2 * row + 1 - core) * high, high)
        grad[pl.ds(here, high), col * wide : (col + 1) * wide] = mine_ref[index]
        grad[pl.ds(there, high), col * wide : (col + 1) * wide] = other_ref[index]

    side = 256
    on_diagonal = lax.broadcasted_iota(jnp.int32, (side, side), 0) == lax.broadcasted_iota(
        jnp.int32, (side, side), 1
    )
    squares = crossed = squared = jnp.zeros((side, side), F32)
    diagonal, rounded = [], []
    for row in range(0, width, side):
        part = grad[row : row + side, :]
        for col in range(row, width, side):
            tile = lax.dot_general(
                part, grad[col : col + side, :], ACROSS, preferred_element_type=F32
            )
            tile_low = tile.astype(LOW)
            back = tile_low.astype(F32)
            tile_rest = (tile - back).astype(LOW)
            stat[row : row + side, col : col + side] = tile_low
            rest[row : row + side, col : col + side] = tile_rest
            if col > row:
                stat[col : col + side, row : row + side] = tile_low.T
                rest[col : col + side, row : row + side] = tile_rest.T
                squares += 2.0 * (tile * tile)
                crossed += tile * back
                squared += back * back
            else:
                outside = jnp.where(on_diagonal, 0.0, back)
                damped = jnp.where(on_diagonal, tile + DAMPING, tile)
                squares += damped * damped
                crossed += 0.5 * (tile * outside)
                squared += 0.5 * (outside * outside)
                diagonal.append(jnp.sum(jnp.where(on_diagonal, tile, 0.0), axis=0, keepdims=True))
                rounded.append(jnp.sum(jnp.where(on_diagonal, back, 0.0), axis=0, keepdims=True))
    inverse = lax.rsqrt(jnp.full((1, 1), jnp.sum(squares), F32))
    above = jnp.full((1, 1), jnp.sum(crossed), F32)
    below = jnp.full((1, 1), jnp.sum(squared), F32)
    gain = jnp.where(below > 0.0, above / jnp.where(below > 0.0, below, 1.0), 1.0)
    delta = DAMPING * inverse
    tau = 1.25 - 0.25 * delta
    own = tau - (0.25 * inverse) * (
        jnp.concatenate(diagonal, axis=1) - gain * jnp.concatenate(rounded, axis=1)
    )
    shared = 0.25 * inverse * gain

    def stepped(vector):
        return own * vector - shared * times(vector, stat[...])

    col_index = lax.broadcasted_iota(jnp.int32, (rows, width), 1)
    row_index = lax.broadcasted_iota(jnp.int32, (rows, width), 0)

    def eye_of(begin):
        return (col_index == begin + row_index).astype(F32)

    def chosen(begin):
        return stat[pl.ds(begin, rows), :].astype(F32) + rest[pl.ds(begin, rows), :].astype(F32)

    eyes = jnp.concatenate([eye_of(begin) for begin in starts], axis=0)
    power = jnp.concatenate([chosen(begin) for begin in starts], axis=0)
    power = (power + DAMPING * eyes) * inverse
    block = pl.multiple_of(start // 128 * 128, 128)
    turned[...] = grad[:, pl.ds(block, 128)].T
    column = turned[pl.ds(pl.multiple_of(start - block, rows), rows), :].astype(F32)
    small = 0.0625 * delta
    square = tau * tau
    factors = [small * (square * tau), small * square, small * tau, small]
    vector = jnp.concatenate([power, column], axis=0)
    inner = (0.3125 - small * (square * square)) * column
    for factor in factors:
        vector = stepped(vector)
        inner -= factor * vector[count:]
    vector = stepped(vector)
    inner += 0.25 * vector[count:]
    left = 1.5625 * eyes - (0.3125 * power + 0.25 * vector[:count])
    keep[...] = left
    rows_ref[:rows, :] = keep[pl.ds(mine, rows), :]

    power = times(left, stat[...]) + jnp.dot(
        left.astype(LOW), rest[...], preferred_element_type=F32
    )
    power = (power + DAMPING * left) * inverse
    vector = power
    for _ in range(5):
        vector = stepped(vector)
    twice = 1.5625 * left - (0.3125 * power + 0.25 * vector)
    out = times(jnp.concatenate([inner, twice], axis=0), grad[...])
    base = 1.5625 - delta * (0.3125 + 0.25 * (square * square * tau))
    rows_ref[rows : 2 * rows, :] = base * eye_of(start) - inverse * out[:rows]
    product = out[rows:]
    total_ref[...] = jnp.full(total_ref.shape, jnp.sum(product * product), F32)
    keep[...] = product
    rows_ref[2 * rows :, :] = keep[pl.ds(mine, rows), :]


def roots(mine, other, rows, devices):
    width = 1024
    vmem = pl.BlockSpec(memory_space=pltpu.VMEM)
    return pl.pallas_call(
        roots_kernel,
        out_shape=(
            jax.ShapeDtypeStruct((3 * rows, width), F32),
            jax.ShapeDtypeStruct((devices, 128), F32),
        ),
        in_specs=[vmem, vmem],
        out_specs=(vmem, vmem),
        scratch_shapes=[
            pltpu.VMEM((width, width), LOW),
            pltpu.VMEM((width, width), LOW),
            pltpu.VMEM((width, width), LOW),
            pltpu.VMEM((128, width), LOW),
            pltpu.VMEM((4 * rows, width), F32),
        ],
        compiler_params=pltpu.CompilerParams(vmem_limit_bytes=32 * 1024 * 1024),
    )(mine, other)


def cut_kernel(got_ref, cols_ref):
    cols_ref[...] = got_ref[:, cols_ref.shape[1] :]


def cut(got):
    vmem = pl.BlockSpec(memory_space=pltpu.VMEM)
    return pl.pallas_call(
        cut_kernel,
        out_shape=jax.ShapeDtypeStruct((got.shape[0], got.shape[1] // 2), LOW),
        in_specs=[vmem],
        out_specs=vmem,
        compiler_params=pltpu.CompilerParams(vmem_limit_bytes=16 * 1024 * 1024),
    )(got)


def against(left, right):
    return lax.dot_general(left, right, (((0,), (0,)), ((), ())), preferred_element_type=F32)


def join_kernel(got_ref, other_ref, mine_ref, tile_ref):
    core = lax.axis_index("core")
    half = mine_ref.shape[0]
    depth, _, rows, columns = tile_ref.shape
    tile_ref[:, core] = mine_ref[...].reshape(depth, rows, columns)
    tile_ref[:, 1 - core] = against(got_ref[:, :half], other_ref[...]).reshape(depth, rows, columns)


def join(got, other, mine, depth):
    vmem = pl.BlockSpec(memory_space=pltpu.VMEM)
    rows, columns = mine.shape
    return pl.pallas_call(
        join_kernel,
        out_shape=jax.ShapeDtypeStruct((depth // 2, 2, rows * 2 // depth, columns), F32),
        in_specs=[vmem, vmem, vmem],
        out_specs=vmem,
        compiler_params=pltpu.CompilerParams(vmem_limit_bytes=16 * 1024 * 1024),
    )(got, other, mine)


def per_device(acts, up_grad):
    tokens, width = acts.shape
    owners = 64
    rows = width // owners
    plane = 8
    depth = 8
    core = lax.axis_index("core")
    halves = [
        lax.dynamic_slice_in_dim(acts, row * 512 + core * 256, 256, 1) for row in range(2)
    ]
    sent = jnp.stack(
        [
            jnp.concatenate([halves[i % 2], up_grad[:, i // 2 * 256 : i // 2 * 256 + 256]], axis=1)
            for i in range(plane)
        ]
    )
    got = lax.all_to_all(sent, PLANE, 0, 0, tiled=True).reshape(plane * tokens, 512)
    swap = [(0, 1), (1, 0)]
    other = lax.ppermute(cut(got), "core", swap)
    tile = join(got, other, against(got[:, :256], got[:, 256:]), depth)
    parts = lax.all_to_all(tile.reshape(depth, 64, 256), DEPTH, 0, 0, tiled=True)
    piece = (jnp.sum(parts, axis=0) / (tokens * owners)).astype(LOW)
    pieces = jnp.broadcast_to(piece[None], (depth // 2, 64, 256))
    tile = lax.all_to_all(pieces, "zh", 0, 0, tiled=True).reshape(256, 256)
    mine = lax.all_to_all(
        jnp.broadcast_to(tile[None], (plane, 256, 256)), PLANE, 0, 0, tiled=True
    )
    other = lax.ppermute(mine, "core", swap)
    found, total = roots(mine, other, rows, 128)
    found = lax.ppermute(found, ("zl", "core"), [(0, 0), (1, 2), (2, 1), (3, 3)])
    totals = lax.all_to_all(total, SPREAD, 0, 0, tiled=True)
    mean = jnp.sum(totals, axis=0, keepdims=True)[:, :1] / (width * width * 8)
    update = found[2 * rows :] * lax.rsqrt(mean + 1e-06)
    return (found[:rows], found[rows : 2 * rows], update)


def solution(mesh):
    fine = Mesh(mesh.devices.reshape(SIZES), NAMES)
    out = P(DP, TENSOR)
    return jax.shard_map(
        per_device,
        mesh=fine,
        in_specs=(P(DP, None), P(DP, TENSOR)),
        out_specs=(out, out, out),
        check_vma=False,
    )
```

```python
import jax
import jax.numpy as jnp
from jax import lax
from jax.experimental import pallas as pl
from jax.experimental.pallas import tpu as pltpu
from jax.sharding import Mesh, PartitionSpec as P

DAMPING = 1e-06
SIZES = (4, 4, 2, 2, 4, 2)
NAMES = ("x", "zh", "zl", "yl", "yh", "core")
DP = ("x", "zh", "zl", "yl")
TENSOR = ("yh", "core")
PLANE = ("x", "yl")
DEPTH = ("zh", "zl")
SPREAD = ("core", "zl", "yl", "x", "yh")
F32 = jnp.float32
LOW = jnp.bfloat16
ACROSS = (((1,), (1,)), ((), ()))


def parts_of(vector):
    high = vector.astype(LOW)
    rest = (vector - high.astype(F32)).astype(LOW)
    return jnp.concatenate([high, rest], axis=0)


def times(vector, weight):
    rows = vector.shape[0]
    both = jnp.dot(parts_of(vector), weight, preferred_element_type=F32)
    return both[:rows] + both[rows:]


def roots_kernel(mine_ref, other_ref, rows_ref, total_ref, grad, stat, rest, turned, keep):
    width = grad.shape[0]
    rows = rows_ref.shape[0] // 3
    n_tiles, high, wide = mine_ref.shape
    groups = keep.shape[0] // rows
    count = groups * rows
    core = lax.axis_index("core")
    first = (lax.axis_index("x") * 16 + core * 2 + lax.axis_index("yl")) * rows
    starts = [pl.multiple_of(first + group * (4 * rows), rows) for group in range(groups)]
    mine = pl.multiple_of(lax.axis_index("zh") * rows, rows)
    start = pl.multiple_of(first + lax.axis_index("zh") * (4 * rows), rows)
    for index in range(n_tiles):
        col, row = index // 2, index % 2
        here = pl.multiple_of((2 * row + core) * high, high)
        there = pl.multiple_of((2 * row + 1 - core) * high, high)
        grad[pl.ds(here, high), col * wide : (col + 1) * wide] = mine_ref[index]
        grad[pl.ds(there, high), col * wide : (col + 1) * wide] = other_ref[index]

    side = 256
    on_diagonal = lax.broadcasted_iota(jnp.int32, (side, side), 0) == lax.broadcasted_iota(
        jnp.int32, (side, side), 1
    )
    squares = crossed = squared = jnp.zeros((side, side), F32)
    diagonal, rounded = [], []
    for row in range(0, width, side):
        part = grad[row : row + side, :]
        for col in range(row, width, side):
            tile = lax.dot_general(
                part, grad[col : col + side, :], ACROSS, preferred_element_type=F32
            )
            tile_low = tile.astype(LOW)
            back = tile_low.astype(F32)
            tile_rest = (tile - back).astype(LOW)
            stat[row : row + side, col : col + side] = tile_low
            rest[row : row + side, col : col + side] = tile_rest
            if col > row:
                stat[col : col + side, row : row + side] = tile_low.T
                rest[col : col + side, row : row + side] = tile_rest.T
                squares += 2.0 * (tile * tile)
                crossed += tile * back
                squared += back * back
            else:
                outside = jnp.where(on_diagonal, 0.0, back)
                damped = jnp.where(on_diagonal, tile + DAMPING, tile)
                squares += damped * damped
                crossed += 0.5 * (tile * outside)
                squared += 0.5 * (outside * outside)
                diagonal.append(jnp.sum(jnp.where(on_diagonal, tile, 0.0), axis=0, keepdims=True))
                rounded.append(jnp.sum(jnp.where(on_diagonal, back, 0.0), axis=0, keepdims=True))
    inverse = lax.rsqrt(jnp.full((1, 1), jnp.sum(squares), F32))
    above = jnp.full((1, 1), jnp.sum(crossed), F32)
    below = jnp.full((1, 1), jnp.sum(squared), F32)
    gain = jnp.where(below > 0.0, above / jnp.where(below > 0.0, below, 1.0), 1.0)
    delta = DAMPING * inverse
    tau = 1.25 - 0.25 * delta
    own = tau - (0.25 * inverse) * (
        jnp.concatenate(diagonal, axis=1) - gain * jnp.concatenate(rounded, axis=1)
    )
    shared = 0.25 * inverse * gain

    def stepped(vector):
        return own * vector - shared * times(vector, stat[...])

    col_index = lax.broadcasted_iota(jnp.int32, (rows, width), 1)
    row_index = lax.broadcasted_iota(jnp.int32, (rows, width), 0)

    def eye_of(begin):
        return (col_index == begin + row_index).astype(F32)

    def chosen(begin):
        return stat[pl.ds(begin, rows), :].astype(F32) + rest[pl.ds(begin, rows), :].astype(F32)

    eyes = jnp.concatenate([eye_of(begin) for begin in starts], axis=0)
    power = jnp.concatenate([chosen(begin) for begin in starts], axis=0)
    power = (power + DAMPING * eyes) * inverse
    block = pl.multiple_of(start // 128 * 128, 128)
    turned[...] = grad[:, pl.ds(block, 128)].T
    column = turned[pl.ds(pl.multiple_of(start - block, rows), rows), :].astype(F32)
    small = 0.0625 * delta
    square = tau * tau
    factors = [small * (square * tau), small * square, small * tau, small]
    vector = jnp.concatenate([power, column], axis=0)
    inner = (0.3125 - small * (square * square)) * column
    for factor in factors:
        vector = stepped(vector)
        inner -= factor * vector[count:]
    vector = stepped(vector)
    inner += 0.25 * vector[count:]
    left = 1.5625 * eyes - (0.3125 * power + 0.25 * vector[:count])
    keep[...] = left
    rows_ref[:rows, :] = keep[pl.ds(mine, rows), :]

    power = times(left, stat[...]) + jnp.dot(
        left.astype(LOW), rest[...], preferred_element_type=F32
    )
    power = (power + DAMPING * left) * inverse
    vector = power
    for _ in range(5):
        vector = stepped(vector)
    twice = 1.5625 * left - (0.3125 * power + 0.25 * vector)
    out = times(jnp.concatenate([inner, twice], axis=0), grad[...])
    base = 1.5625 - delta * (0.3125 + 0.25 * (square * square * tau))
    rows_ref[rows : 2 * rows, :] = base * eye_of(start) - inverse * out[:rows]
    product = out[rows:]
    total_ref[...] = jnp.full(total_ref.shape, jnp.sum(product * product), F32)
    keep[...] = product
    rows_ref[2 * rows :, :] = keep[pl.ds(mine, rows), :]


def roots(mine, other, rows, devices):
    width = 1024
    vmem = pl.BlockSpec(memory_space=pltpu.VMEM)
    return pl.pallas_call(
        roots_kernel,
        out_shape=(
            jax.ShapeDtypeStruct((3 * rows, width), F32),
            jax.ShapeDtypeStruct((devices, 128), F32),
        ),
        in_specs=[vmem, vmem],
        out_specs=(vmem, vmem),
        scratch_shapes=[
            pltpu.VMEM((width, width), LOW),
            pltpu.VMEM((width, width), LOW),
            pltpu.VMEM((width, width), LOW),
            pltpu.VMEM((128, width), LOW),
            pltpu.VMEM((4 * rows, width), F32),
        ],
        compiler_params=pltpu.CompilerParams(vmem_limit_bytes=32 * 1024 * 1024),
    )(mine, other)


def cut_kernel(got_ref, cols_ref):
    half = cols_ref.shape[1]
    cols_ref[...] = got_ref[:, half:, :].reshape(cols_ref.shape)


def cut(got):
    vmem = pl.BlockSpec(memory_space=pltpu.VMEM)
    senders, both, columns = got.shape
    return pl.pallas_call(
        cut_kernel,
        out_shape=jax.ShapeDtypeStruct((senders * both // 2, columns), LOW),
        in_specs=[vmem],
        out_specs=vmem,
        compiler_params=pltpu.CompilerParams(vmem_limit_bytes=16 * 1024 * 1024),
    )(got)


def against(left, right):
    return lax.dot_general(left, right, (((0,), (0,)), ((), ())), preferred_element_type=F32)


def own_kernel(got_ref, mine_ref):
    half, columns = mine_ref.shape
    left = got_ref[:, :half, :].reshape(-1, columns)
    right = got_ref[:, half:, :].reshape(-1, columns)
    mine_ref[...] = against(left, right)


def own(got):
    vmem = pl.BlockSpec(memory_space=pltpu.VMEM)
    _, both, columns = got.shape
    return pl.pallas_call(
        own_kernel,
        out_shape=jax.ShapeDtypeStruct((both // 2, columns), F32),
        in_specs=[vmem],
        out_specs=vmem,
        compiler_params=pltpu.CompilerParams(vmem_limit_bytes=16 * 1024 * 1024),
        cost_estimate=pl.CostEstimate(flops=2**28, bytes_accessed=2**21, transcendentals=0),
    )(got)


def join_kernel(got_ref, other_ref, mine_ref, tile_ref):
    core = lax.axis_index("core")
    half = mine_ref.shape[0]
    depth, _, rows, columns = tile_ref.shape
    left = got_ref[:, :half, :].reshape(-1, columns)
    tile_ref[:, core] = mine_ref[...].reshape(depth, rows, columns)
    tile_ref[:, 1 - core] = against(left, other_ref[...]).reshape(depth, rows, columns)


def join(got, other, mine, depth):
    vmem = pl.BlockSpec(memory_space=pltpu.VMEM)
    rows, columns = mine.shape
    return pl.pallas_call(
        join_kernel,
        out_shape=jax.ShapeDtypeStruct((depth // 2, 2, rows * 2 // depth, columns), F32),
        in_specs=[vmem, vmem, vmem],
        out_specs=vmem,
        compiler_params=pltpu.CompilerParams(vmem_limit_bytes=16 * 1024 * 1024),
    )(got, other, mine)


def per_device(acts, up_grad):
    tokens, width = acts.shape
    owners = 64
    rows = width // owners
    plane = 8
    depth = 8
    core = lax.axis_index("core")
    halves = [
        lax.dynamic_slice_in_dim(acts, row * 512 + core * 256, 256, 1) for row in range(2)
    ]
    sent = jnp.stack(
        [
            jnp.concatenate([halves[i % 2], up_grad[:, i // 2 * 256 : i // 2 * 256 + 256]], axis=0)
            for i in range(plane)
        ]
    )
    got = lax.all_to_all(sent, PLANE, 0, 0, tiled=True)
    swap = [(0, 1), (1, 0)]
    other = lax.ppermute(cut(got), "core", swap)
    tile = join(got, other, own(got), depth)
    parts = lax.all_to_all(tile.reshape(depth, 64, 256), DEPTH, 0, 0, tiled=True)
    piece = (jnp.sum(parts, axis=0) / (tokens * owners)).astype(LOW)
    pieces = jnp.broadcast_to(piece[None], (depth // 2, 64, 256))
    tile = lax.all_to_all(pieces, "zh", 0, 0, tiled=True).reshape(256, 256)
    mine = lax.all_to_all(
        jnp.broadcast_to(tile[None], (plane, 256, 256)), PLANE, 0, 0, tiled=True
    )
    other = lax.ppermute(mine, "core", swap)
    found, total = roots(mine, other, rows, 128)
    found = lax.ppermute(found, ("zl", "core"), [(0, 0), (1, 2), (2, 1), (3, 3)])
    totals = lax.all_to_all(total, SPREAD, 0, 0, tiled=True)
    mean = jnp.sum(totals, axis=0, keepdims=True)[:, :1] / (width * width * 8)
    update = found[2 * rows :] * lax.rsqrt(mean + 1e-06)
    return (found[:rows], found[rows : 2 * rows], update)


def solution(mesh):
    fine = Mesh(mesh.devices.reshape(SIZES), NAMES)
    out = P(DP, TENSOR)
    return jax.shard_map(
        per_device,
        mesh=fine,
        in_specs=(P(DP, None), P(DP, TENSOR)),
        out_specs=(out, out, out),
        check_vma=False,
    )
```

```python
import jax
import jax.numpy as jnp
from jax import lax
from jax.experimental import pallas as pl
from jax.experimental.pallas import tpu as pltpu
from jax.sharding import Mesh, PartitionSpec as P

DAMPING = 1e-06
SIZES = (4, 4, 2, 2, 4, 2)
NAMES = ("x", "zh", "zl", "yl", "yh", "core")
DP = ("x", "zh", "zl", "yl")
TENSOR = ("yh", "core")
PLANE = ("x", "yl")
DEPTH = ("zl", "zh")
SPREAD = ("core", "zl", "yl", "x", "yh")
F32 = jnp.float32
LOW = jnp.bfloat16
ACROSS = (((1,), (1,)), ((), ()))


def parts_of(vector):
    high = vector.astype(LOW)
    rest = (vector - high.astype(F32)).astype(LOW)
    return jnp.concatenate([high, rest], axis=0)


def times(vector, weight):
    rows = vector.shape[0]
    both = jnp.dot(parts_of(vector), weight, preferred_element_type=F32)
    return both[:rows] + both[rows:]


def roots_kernel(mine_ref, other_ref, rows_ref, total_ref, grad, stat, rest, turned, keep):
    width = grad.shape[0]
    rows = rows_ref.shape[0] // 3
    n_tiles, high, wide = mine_ref.shape
    groups = keep.shape[0] // rows
    count = groups * rows
    core = lax.axis_index("core")
    first = (lax.axis_index("x") * 16 + core * 2 + lax.axis_index("yl")) * rows
    starts = [pl.multiple_of(first + group * (4 * rows), rows) for group in range(groups)]
    mine = pl.multiple_of(lax.axis_index("zh") * rows, rows)
    start = pl.multiple_of(first + lax.axis_index("zh") * (4 * rows), rows)
    for index in range(n_tiles):
        col, row = index // 2, index % 2
        here = pl.multiple_of((2 * row + core) * high, high)
        there = pl.multiple_of((2 * row + 1 - core) * high, high)
        grad[pl.ds(here, high), col * wide : (col + 1) * wide] = mine_ref[index]
        grad[pl.ds(there, high), col * wide : (col + 1) * wide] = other_ref[index]

    side = 256
    on_diagonal = lax.broadcasted_iota(jnp.int32, (side, side), 0) == lax.broadcasted_iota(
        jnp.int32, (side, side), 1
    )
    squares = crossed = squared = jnp.zeros((side, side), F32)
    diagonal, rounded = [], []
    for row in range(0, width, side):
        part = grad[row : row + side, :]
        for col in range(row, width, side):
            tile = lax.dot_general(
                part, grad[col : col + side, :], ACROSS, preferred_element_type=F32
            )
            tile_low = tile.astype(LOW)
            back = tile_low.astype(F32)
            tile_rest = (tile - back).astype(LOW)
            stat[row : row + side, col : col + side] = tile_low
            rest[row : row + side, col : col + side] = tile_rest
            if col > row:
                stat[col : col + side, row : row + side] = tile_low.T
                rest[col : col + side, row : row + side] = tile_rest.T
                squares += 2.0 * (tile * tile)
                crossed += tile * back
                squared += back * back
            else:
                outside = jnp.where(on_diagonal, 0.0, back)
                damped = jnp.where(on_diagonal, tile + DAMPING, tile)
                squares += damped * damped
                crossed += 0.5 * (tile * outside)
                squared += 0.5 * (outside * outside)
                diagonal.append(jnp.sum(jnp.where(on_diagonal, tile, 0.0), axis=0, keepdims=True))
                rounded.append(jnp.sum(jnp.where(on_diagonal, back, 0.0), axis=0, keepdims=True))
    inverse = lax.rsqrt(jnp.full((1, 1), jnp.sum(squares), F32))
    above = jnp.full((1, 1), jnp.sum(crossed), F32)
    below = jnp.full((1, 1), jnp.sum(squared), F32)
    gain = jnp.where(below > 0.0, above / jnp.where(below > 0.0, below, 1.0), 1.0)
    delta = DAMPING * inverse
    tau = 1.25 - 0.25 * delta
    own = tau - (0.25 * inverse) * (
        jnp.concatenate(diagonal, axis=1) - gain * jnp.concatenate(rounded, axis=1)
    )
    shared = 0.25 * inverse * gain

    def stepped(vector):
        return own * vector - shared * times(vector, stat[...])

    col_index = lax.broadcasted_iota(jnp.int32, (rows, width), 1)
    row_index = lax.broadcasted_iota(jnp.int32, (rows, width), 0)

    def eye_of(begin):
        return (col_index == begin + row_index).astype(F32)

    def chosen(begin):
        return stat[pl.ds(begin, rows), :].astype(F32) + rest[pl.ds(begin, rows), :].astype(F32)

    eyes = jnp.concatenate([eye_of(begin) for begin in starts], axis=0)
    power = jnp.concatenate([chosen(begin) for begin in starts], axis=0)
    power = (power + DAMPING * eyes) * inverse
    block = pl.multiple_of(start // 128 * 128, 128)
    turned[...] = grad[:, pl.ds(block, 128)].T
    column = turned[pl.ds(pl.multiple_of(start - block, rows), rows), :].astype(F32)
    small = 0.0625 * delta
    square = tau * tau
    factors = [small * (square * tau), small * square, small * tau, small]
    vector = jnp.concatenate([power, column], axis=0)
    inner = (0.3125 - small * (square * square)) * column
    for factor in factors:
        vector = stepped(vector)
        inner -= factor * vector[count:]
    vector = stepped(vector)
    inner += 0.25 * vector[count:]
    left = 1.5625 * eyes - (0.3125 * power + 0.25 * vector[:count])
    keep[...] = left
    rows_ref[:rows, :] = keep[pl.ds(mine, rows), :]

    power = times(left, stat[...]) + jnp.dot(
        left.astype(LOW), rest[...], preferred_element_type=F32
    )
    power = (power + DAMPING * left) * inverse
    vector = power
    for _ in range(5):
        vector = stepped(vector)
    twice = 1.5625 * left - (0.3125 * power + 0.25 * vector)
    out = times(jnp.concatenate([inner, twice], axis=0), grad[...])
    base = 1.5625 - delta * (0.3125 + 0.25 * (square * square * tau))
    rows_ref[rows : 2 * rows, :] = base * eye_of(start) - inverse * out[:rows]
    product = out[rows:]
    total_ref[...] = jnp.full(total_ref.shape, jnp.sum(product * product), F32)
    keep[...] = product
    rows_ref[2 * rows :, :] = keep[pl.ds(mine, rows), :]


def roots(mine, other, rows, devices):
    width = 1024
    vmem = pl.BlockSpec(memory_space=pltpu.VMEM)
    return pl.pallas_call(
        roots_kernel,
        out_shape=(
            jax.ShapeDtypeStruct((3 * rows, width), F32),
            jax.ShapeDtypeStruct((devices, 128), F32),
        ),
        in_specs=[vmem, vmem],
        out_specs=(vmem, vmem),
        scratch_shapes=[
            pltpu.VMEM((width, width), LOW),
            pltpu.VMEM((width, width), LOW),
            pltpu.VMEM((width, width), LOW),
            pltpu.VMEM((128, width), LOW),
            pltpu.VMEM((4 * rows, width), F32),
        ],
        compiler_params=pltpu.CompilerParams(vmem_limit_bytes=32 * 1024 * 1024),
    )(mine, other)


def cut_kernel(got_ref, cols_ref):
    half = cols_ref.shape[1]
    cols_ref[...] = got_ref[:, half:, :].reshape(cols_ref.shape)


def cut(got):
    vmem = pl.BlockSpec(memory_space=pltpu.VMEM)
    senders, both, columns = got.shape
    return pl.pallas_call(
        cut_kernel,
        out_shape=jax.ShapeDtypeStruct((senders * both // 2, columns), LOW),
        in_specs=[vmem],
        out_specs=vmem,
        compiler_params=pltpu.CompilerParams(vmem_limit_bytes=16 * 1024 * 1024),
    )(got)


def against(left, right):
    return lax.dot_general(left, right, (((0,), (0,)), ((), ())), preferred_element_type=F32)


def own_kernel(got_ref, mine_ref):
    half, columns = mine_ref.shape
    left = got_ref[:, :half, :].reshape(-1, columns)
    right = got_ref[:, half:, :].reshape(-1, columns)
    mine_ref[...] = against(left, right)


def own(got):
    vmem = pl.BlockSpec(memory_space=pltpu.VMEM)
    _, both, columns = got.shape
    return pl.pallas_call(
        own_kernel,
        out_shape=jax.ShapeDtypeStruct((both // 2, columns), F32),
        in_specs=[vmem],
        out_specs=vmem,
        compiler_params=pltpu.CompilerParams(vmem_limit_bytes=16 * 1024 * 1024),
        cost_estimate=pl.CostEstimate(flops=2**28, bytes_accessed=2**21, transcendentals=0),
    )(got)


def join_kernel(got_ref, other_ref, mine_ref, tile_ref):
    core = lax.axis_index("core")
    half = mine_ref.shape[0]
    _, depth, rows, columns = tile_ref.shape
    left = got_ref[:, :half, :].reshape(-1, columns)
    tile_ref[core] = mine_ref[...].reshape(depth, rows, columns)
    tile_ref[1 - core] = against(left, other_ref[...]).reshape(depth, rows, columns)


def join(got, other, mine, depth):
    vmem = pl.BlockSpec(memory_space=pltpu.VMEM)
    rows, columns = mine.shape
    return pl.pallas_call(
        join_kernel,
        out_shape=jax.ShapeDtypeStruct((2, depth // 2, rows * 2 // depth, columns), F32),
        in_specs=[vmem, vmem, vmem],
        out_specs=vmem,
        compiler_params=pltpu.CompilerParams(vmem_limit_bytes=16 * 1024 * 1024),
    )(got, other, mine)


def per_device(acts, up_grad):
    tokens, width = acts.shape
    owners = 64
    rows = width // owners
    plane = 8
    depth = 8
    core = lax.axis_index("core")
    halves = [
        lax.dynamic_slice_in_dim(acts, row * 512 + core * 256, 256, 1) for row in range(2)
    ]
    sent = jnp.stack(
        [
            jnp.concatenate([halves[i % 2], up_grad[:, i // 2 * 256 : i // 2 * 256 + 256]], axis=0)
            for i in range(plane)
        ]
    )
    got = lax.all_to_all(sent, PLANE, 0, 0, tiled=True)
    swap = [(0, 1), (1, 0)]
    other = lax.ppermute(cut(got), "core", swap)
    tile = join(got, other, own(got), depth)
    parts = lax.all_to_all(tile.reshape(depth, 64, 256), DEPTH, 0, 0, tiled=True)
    piece = (jnp.sum(parts, axis=0) / (tokens * owners)).astype(LOW)
    pieces = jnp.broadcast_to(piece[None], (depth // 2, 64, 256))
    tile = lax.all_to_all(pieces, "zh", 0, 0, tiled=True).reshape(256, 256)
    mine = lax.all_to_all(
        jnp.broadcast_to(tile[None], (plane, 256, 256)), PLANE, 0, 0, tiled=True
    )
    other = lax.ppermute(mine, "core", swap)
    found, total = roots(mine, other, rows, 128)
    found = lax.ppermute(found, ("zl", "core"), [(0, 0), (1, 2), (2, 1), (3, 3)])
    totals = lax.all_to_all(total, SPREAD, 0, 0, tiled=True)
    mean = jnp.sum(totals, axis=0, keepdims=True)[:, :1] / (width * width * 8)
    update = found[2 * rows :] * lax.rsqrt(mean + 1e-06)
    return (found[:rows], found[rows : 2 * rows], update)


def solution(mesh):
    fine = Mesh(mesh.devices.reshape(SIZES), NAMES)
    out = P(DP, TENSOR)
    return jax.shard_map(
        per_device,
        mesh=fine,
        in_specs=(P(DP, None), P(DP, TENSOR)),
        out_specs=(out, out, out),
        check_vma=False,
    )
```

```python
import jax
import jax.numpy as jnp
from jax import lax
from jax.experimental import pallas as pl
from jax.experimental.pallas import tpu as pltpu
from jax.sharding import Mesh, PartitionSpec as P

DAMPING = 1e-06
SIZES = (4, 4, 2, 2, 4, 2)
NAMES = ("x", "zh", "zl", "yl", "yh", "core")
DP = ("x", "zh", "zl", "yl")
TENSOR = ("yh", "core")
PLANE = ("yl", "x")
DEPTH = ("zl", "zh")
SPREAD = ("core", "zl", "yl", "x", "yh")
F32 = jnp.float32
LOW = jnp.bfloat16
ACROSS = (((1,), (1,)), ((), ()))


def parts_of(vector):
    high = vector.astype(LOW)
    rest = (vector - high.astype(F32)).astype(LOW)
    return jnp.concatenate([high, rest], axis=0)


def times(vector, weight):
    rows = vector.shape[0]
    both = jnp.dot(parts_of(vector), weight, preferred_element_type=F32)
    return both[:rows] + both[rows:]


def roots_kernel(mine_ref, other_ref, rows_ref, total_ref, grad, stat, rest, turned, keep):
    width = grad.shape[0]
    rows = rows_ref.shape[0] // 3
    n_tiles, high, wide = mine_ref.shape
    groups = keep.shape[0] // rows
    count = groups * rows
    core = lax.axis_index("core")
    first = (lax.axis_index("x") * 16 + core * 2 + lax.axis_index("yl")) * rows
    starts = [pl.multiple_of(first + group * (4 * rows), rows) for group in range(groups)]
    mine = pl.multiple_of(lax.axis_index("zh") * rows, rows)
    start = pl.multiple_of(first + lax.axis_index("zh") * (4 * rows), rows)
    for index in range(n_tiles):
        row, col = index // 4, index % 4
        here = pl.multiple_of((2 * row + core) * high, high)
        there = pl.multiple_of((2 * row + 1 - core) * high, high)
        grad[pl.ds(here, high), col * wide : (col + 1) * wide] = mine_ref[index]
        grad[pl.ds(there, high), col * wide : (col + 1) * wide] = other_ref[index]

    side = 256
    on_diagonal = lax.broadcasted_iota(jnp.int32, (side, side), 0) == lax.broadcasted_iota(
        jnp.int32, (side, side), 1
    )
    squares = crossed = squared = jnp.zeros((side, side), F32)
    diagonal, rounded = [], []
    for row in range(0, width, side):
        part = grad[row : row + side, :]
        for col in range(row, width, side):
            tile = lax.dot_general(
                part, grad[col : col + side, :], ACROSS, preferred_element_type=F32
            )
            tile_low = tile.astype(LOW)
            back = tile_low.astype(F32)
            tile_rest = (tile - back).astype(LOW)
            stat[row : row + side, col : col + side] = tile_low
            rest[row : row + side, col : col + side] = tile_rest
            if col > row:
                stat[col : col + side, row : row + side] = tile_low.T
                rest[col : col + side, row : row + side] = tile_rest.T
                squares += 2.0 * (tile * tile)
                crossed += tile * back
                squared += back * back
            else:
                outside = jnp.where(on_diagonal, 0.0, back)
                damped = jnp.where(on_diagonal, tile + DAMPING, tile)
                squares += damped * damped
                crossed += 0.5 * (tile * outside)
                squared += 0.5 * (outside * outside)
                diagonal.append(jnp.sum(jnp.where(on_diagonal, tile, 0.0), axis=0, keepdims=True))
                rounded.append(jnp.sum(jnp.where(on_diagonal, back, 0.0), axis=0, keepdims=True))
    inverse = lax.rsqrt(jnp.full((1, 1), jnp.sum(squares), F32))
    above = jnp.full((1, 1), jnp.sum(crossed), F32)
    below = jnp.full((1, 1), jnp.sum(squared), F32)
    gain = jnp.where(below > 0.0, above / jnp.where(below > 0.0, below, 1.0), 1.0)
    delta = DAMPING * inverse
    tau = 1.25 - 0.25 * delta
    own = tau - (0.25 * inverse) * (
        jnp.concatenate(diagonal, axis=1) - gain * jnp.concatenate(rounded, axis=1)
    )
    shared = 0.25 * inverse * gain

    def stepped(vector):
        return own * vector - shared * times(vector, stat[...])

    col_index = lax.broadcasted_iota(jnp.int32, (rows, width), 1)
    row_index = lax.broadcasted_iota(jnp.int32, (rows, width), 0)

    def eye_of(begin):
        return (col_index == begin + row_index).astype(F32)

    def chosen(begin):
        return stat[pl.ds(begin, rows), :].astype(F32) + rest[pl.ds(begin, rows), :].astype(F32)

    eyes = jnp.concatenate([eye_of(begin) for begin in starts], axis=0)
    power = jnp.concatenate([chosen(begin) for begin in starts], axis=0)
    power = (power + DAMPING * eyes) * inverse
    block = pl.multiple_of(start // 128 * 128, 128)
    turned[...] = grad[:, pl.ds(block, 128)].T
    column = turned[pl.ds(pl.multiple_of(start - block, rows), rows), :].astype(F32)
    small = 0.0625 * delta
    square = tau * tau
    factors = [small * (square * tau), small * square, small * tau, small]
    vector = jnp.concatenate([power, column], axis=0)
    inner = (0.3125 - small * (square * square)) * column
    for factor in factors:
        vector = stepped(vector)
        inner -= factor * vector[count:]
    vector = stepped(vector)
    inner += 0.25 * vector[count:]
    left = 1.5625 * eyes - (0.3125 * power + 0.25 * vector[:count])
    keep[...] = left
    rows_ref[:rows, :] = keep[pl.ds(mine, rows), :]

    power = times(left, stat[...]) + jnp.dot(
        left.astype(LOW), rest[...], preferred_element_type=F32
    )
    power = (power + DAMPING * left) * inverse
    vector = power
    for _ in range(5):
        vector = stepped(vector)
    twice = 1.5625 * left - (0.3125 * power + 0.25 * vector)
    out = times(jnp.concatenate([inner, twice], axis=0), grad[...])
    base = 1.5625 - delta * (0.3125 + 0.25 * (square * square * tau))
    rows_ref[rows : 2 * rows, :] = base * eye_of(start) - inverse * out[:rows]
    product = out[rows:]
    total_ref[...] = jnp.full(total_ref.shape, jnp.sum(product * product), F32)
    keep[...] = product
    rows_ref[2 * rows :, :] = keep[pl.ds(mine, rows), :]


def roots(mine, other, rows, devices):
    width = 1024
    vmem = pl.BlockSpec(memory_space=pltpu.VMEM)
    return pl.pallas_call(
        roots_kernel,
        out_shape=(
            jax.ShapeDtypeStruct((3 * rows, width), F32),
            jax.ShapeDtypeStruct((devices, 128), F32),
        ),
        in_specs=[vmem, vmem],
        out_specs=(vmem, vmem),
        scratch_shapes=[
            pltpu.VMEM((width, width), LOW),
            pltpu.VMEM((width, width), LOW),
            pltpu.VMEM((width, width), LOW),
            pltpu.VMEM((128, width), LOW),
            pltpu.VMEM((4 * rows, width), F32),
        ],
        compiler_params=pltpu.CompilerParams(vmem_limit_bytes=32 * 1024 * 1024),
    )(mine, other)


def cut_kernel(got_ref, cols_ref):
    half = cols_ref.shape[1]
    cols_ref[...] = got_ref[:, half:, :].reshape(cols_ref.shape)


def cut(got):
    vmem = pl.BlockSpec(memory_space=pltpu.VMEM)
    senders, both, columns = got.shape
    return pl.pallas_call(
        cut_kernel,
        out_shape=jax.ShapeDtypeStruct((senders * both // 2, columns), LOW),
        in_specs=[vmem],
        out_specs=vmem,
        compiler_params=pltpu.CompilerParams(vmem_limit_bytes=16 * 1024 * 1024),
    )(got)


def against(left, right):
    return lax.dot_general(left, right, (((0,), (0,)), ((), ())), preferred_element_type=F32)


def own_kernel(got_ref, mine_ref):
    half, columns = mine_ref.shape
    left = got_ref[:, :half, :].reshape(-1, columns)
    right = got_ref[:, half:, :].reshape(-1, columns)
    mine_ref[...] = against(left, right)


def own(got):
    vmem = pl.BlockSpec(memory_space=pltpu.VMEM)
    _, both, columns = got.shape
    return pl.pallas_call(
        own_kernel,
        out_shape=jax.ShapeDtypeStruct((both // 2, columns), F32),
        in_specs=[vmem],
        out_specs=vmem,
        compiler_params=pltpu.CompilerParams(vmem_limit_bytes=16 * 1024 * 1024),
        cost_estimate=pl.CostEstimate(flops=2**28, bytes_accessed=2**21, transcendentals=0),
    )(got)


def join_kernel(got_ref, other_ref, mine_ref, tile_ref):
    core = lax.axis_index("core")
    half = mine_ref.shape[0]
    _, depth, rows, columns = tile_ref.shape
    left = got_ref[:, :half, :].reshape(-1, columns)
    tile_ref[core] = mine_ref[...].reshape(depth, rows, columns)
    tile_ref[1 - core] = against(left, other_ref[...]).reshape(depth, rows, columns)


def join(got, other, mine, depth):
    vmem = pl.BlockSpec(memory_space=pltpu.VMEM)
    rows, columns = mine.shape
    return pl.pallas_call(
        join_kernel,
        out_shape=jax.ShapeDtypeStruct((2, depth // 2, rows * 2 // depth, columns), F32),
        in_specs=[vmem, vmem, vmem],
        out_specs=vmem,
        compiler_params=pltpu.CompilerParams(vmem_limit_bytes=16 * 1024 * 1024),
    )(got, other, mine)


def per_device(acts, up_grad):
    tokens, width = acts.shape
    owners = 64
    rows = width // owners
    plane = 8
    depth = 8
    core = lax.axis_index("core")
    halves = [
        lax.dynamic_slice_in_dim(acts, row * 512 + core * 256, 256, 1) for row in range(2)
    ]
    sent = jnp.stack(
        [
            jnp.concatenate([halves[i // 4], up_grad[:, i % 4 * 256 : i % 4 * 256 + 256]], axis=0)
            for i in range(plane)
        ]
    )
    got = lax.all_to_all(sent, PLANE, 0, 0, tiled=True)
    swap = [(0, 1), (1, 0)]
    other = lax.ppermute(cut(got), "core", swap)
    tile = join(got, other, own(got), depth)
    parts = lax.all_to_all(tile.reshape(depth, 64, 256), DEPTH, 0, 0, tiled=True)
    piece = (jnp.sum(parts, axis=0) / (tokens * owners)).astype(LOW)
    pieces = jnp.broadcast_to(piece[None], (depth // 2, 64, 256))
    tile = lax.all_to_all(pieces, "zh", 0, 0, tiled=True).reshape(256, 256)
    mine = lax.all_to_all(
        jnp.broadcast_to(tile[None], (plane, 256, 256)), PLANE, 0, 0, tiled=True
    )
    other = lax.ppermute(mine, "core", swap)
    found, total = roots(mine, other, rows, 128)
    found = lax.ppermute(found, ("zl", "core"), [(0, 0), (1, 2), (2, 1), (3, 3)])
    totals = lax.all_to_all(total, SPREAD, 0, 0, tiled=True)
    mean = jnp.sum(totals, axis=0, keepdims=True)[:, :1] / (width * width * 8)
    update = found[2 * rows :] * lax.rsqrt(mean + 1e-06)
    return (found[:rows], found[rows : 2 * rows], update)


def solution(mesh):
    fine = Mesh(mesh.devices.reshape(SIZES), NAMES)
    out = P(DP, TENSOR)
    return jax.shard_map(
        per_device,
        mesh=fine,
        in_specs=(P(DP, None), P(DP, TENSOR)),
        out_specs=(out, out, out),
        check_vma=False,
    )
```

```python
import jax
import jax.numpy as jnp
from jax import lax
from jax.experimental import pallas as pl
from jax.experimental.pallas import tpu as pltpu
from jax.sharding import Mesh, PartitionSpec as P

DAMPING = 1e-06
SIZES = (4, 4, 2, 2, 4, 2)
NAMES = ("x", "zh", "zl", "yl", "yh", "core")
DP = ("x", "zh", "zl", "yl")
TENSOR = ("yh", "core")
PLANE = ("yl", "x")
DEPTH = ("zl", "zh")
SPREAD = ("core", "zl", "yl", "x", "yh")
F32 = jnp.float32
LOW = jnp.bfloat16
ACROSS = (((1,), (1,)), ((), ()))


def parts_of(vector):
    high = vector.astype(LOW)
    rest = (vector - high.astype(F32)).astype(LOW)
    return jnp.concatenate([high, rest], axis=0)


def times(vector, weight):
    rows = vector.shape[0]
    both = jnp.dot(parts_of(vector), weight, preferred_element_type=F32)
    return both[:rows] + both[rows:]


def roots_kernel(mine_ref, other_ref, rows_ref, total_ref, grad, stat, rest, turned, keep):
    width = grad.shape[0]
    rows = rows_ref.shape[0] // 3
    n_tiles, high, wide = mine_ref.shape
    groups = keep.shape[0] // rows
    count = groups * rows
    core = lax.axis_index("core")
    first = (lax.axis_index("x") * 16 + core * 2 + lax.axis_index("yl")) * rows
    starts = [pl.multiple_of(first + group * (4 * rows), rows) for group in range(groups)]
    mine = pl.multiple_of(lax.axis_index("zh") * rows, rows)
    start = pl.multiple_of(first + lax.axis_index("zh") * (4 * rows), rows)
    for index in range(n_tiles):
        row, col = index // 4, index % 4
        here = pl.multiple_of((2 * row + core) * high, high)
        there = pl.multiple_of((2 * row + 1 - core) * high, high)
        grad[pl.ds(here, high), col * wide : (col + 1) * wide] = mine_ref[index]
        grad[pl.ds(there, high), col * wide : (col + 1) * wide] = other_ref[index]

    side = 256
    on_diagonal = lax.broadcasted_iota(jnp.int32, (side, side), 0) == lax.broadcasted_iota(
        jnp.int32, (side, side), 1
    )
    squares = crossed = squared = jnp.zeros((side, side), F32)
    squares_on = crossed_on = squared_on = squares
    diagonal, rounded = [], []
    for row in range(0, width, side):
        part = grad[row : row + side, :]
        for col in range(row, width, side):
            tile = lax.dot_general(
                part, grad[col : col + side, :], ACROSS, preferred_element_type=F32
            )
            tile_low = tile.astype(LOW)
            back = tile_low.astype(F32)
            tile_rest = (tile - back).astype(LOW)
            stat[row : row + side, col : col + side] = tile_low
            rest[row : row + side, col : col + side] = tile_rest
            if col > row:
                stat[col : col + side, row : row + side] = tile_low.T
                rest[col : col + side, row : row + side] = tile_rest.T
                squares += tile * tile
                crossed += tile * back
                squared += back * back
            else:
                outside = jnp.where(on_diagonal, 0.0, back)
                damped = jnp.where(on_diagonal, tile + DAMPING, tile)
                squares_on += damped * damped
                crossed_on += tile * outside
                squared_on += outside * outside
                diagonal.append(jnp.sum(jnp.where(on_diagonal, tile, 0.0), axis=0, keepdims=True))
                rounded.append(jnp.sum(jnp.where(on_diagonal, back, 0.0), axis=0, keepdims=True))
    inverse = lax.rsqrt(jnp.full((1, 1), jnp.sum(2.0 * squares + squares_on), F32))
    above = jnp.full((1, 1), jnp.sum(2.0 * crossed + crossed_on), F32)
    below = jnp.full((1, 1), jnp.sum(2.0 * squared + squared_on), F32)
    gain = jnp.where(below > 0.0, above / jnp.where(below > 0.0, below, 1.0), 1.0)
    delta = DAMPING * inverse
    tau = 1.25 - 0.25 * delta
    own = tau - (0.25 * inverse) * (
        jnp.concatenate(diagonal, axis=1) - gain * jnp.concatenate(rounded, axis=1)
    )
    shared = 0.25 * inverse * gain

    def stepped(vector):
        return own * vector - shared * times(vector, stat[...])

    col_index = lax.broadcasted_iota(jnp.int32, (rows, width), 1)
    row_index = lax.broadcasted_iota(jnp.int32, (rows, width), 0)

    def eye_of(begin):
        return (col_index == begin + row_index).astype(F32)

    def chosen(begin):
        return stat[pl.ds(begin, rows), :].astype(F32) + rest[pl.ds(begin, rows), :].astype(F32)

    eyes = jnp.concatenate([eye_of(begin) for begin in starts], axis=0)
    power = jnp.concatenate([chosen(begin) for begin in starts], axis=0)
    power = (power + DAMPING * eyes) * inverse
    block = pl.multiple_of(start // 128 * 128, 128)
    turned[...] = grad[:, pl.ds(block, 128)].T
    column = turned[pl.ds(pl.multiple_of(start - block, rows), rows), :].astype(F32)
    small = 0.0625 * delta
    square = tau * tau
    factors = [small * (square * tau), small * square, small * tau, small]
    vector = jnp.concatenate([power, column], axis=0)
    inner = (0.3125 - small * (square * square)) * column
    for factor in factors:
        vector = stepped(vector)
        inner -= factor * vector[count:]
    vector = stepped(vector)
    inner += 0.25 * vector[count:]
    left = 1.5625 * eyes - (0.3125 * power + 0.25 * vector[:count])
    keep[...] = left
    rows_ref[:rows, :] = keep[pl.ds(mine, rows), :]

    power = times(left, stat[...]) + jnp.dot(
        left.astype(LOW), rest[...], preferred_element_type=F32
    )
    power = (power + DAMPING * left) * inverse
    vector = power
    for _ in range(5):
        vector = stepped(vector)
    twice = 1.5625 * left - (0.3125 * power + 0.25 * vector)
    out = times(jnp.concatenate([inner, twice], axis=0), grad[...])
    base = 1.5625 - delta * (0.3125 + 0.25 * (square * square * tau))
    rows_ref[rows : 2 * rows, :] = base * eye_of(start) - inverse * out[:rows]
    product = out[rows:]
    total_ref[...] = jnp.full(total_ref.shape, jnp.sum(product * product), F32)
    keep[...] = product
    rows_ref[2 * rows :, :] = keep[pl.ds(mine, rows), :]


def roots(mine, other, rows, devices):
    width = 1024
    vmem = pl.BlockSpec(memory_space=pltpu.VMEM)
    return pl.pallas_call(
        roots_kernel,
        out_shape=(
            jax.ShapeDtypeStruct((3 * rows, width), F32),
            jax.ShapeDtypeStruct((devices, 128), F32),
        ),
        in_specs=[vmem, vmem],
        out_specs=(vmem, vmem),
        scratch_shapes=[
            pltpu.VMEM((width, width), LOW),
            pltpu.VMEM((width, width), LOW),
            pltpu.VMEM((width, width), LOW),
            pltpu.VMEM((128, width), LOW),
            pltpu.VMEM((4 * rows, width), F32),
        ],
        compiler_params=pltpu.CompilerParams(vmem_limit_bytes=32 * 1024 * 1024),
    )(mine, other)


def cut_kernel(got_ref, cols_ref):
    half = cols_ref.shape[1]
    cols_ref[...] = got_ref[:, half:, :].reshape(cols_ref.shape)


def cut(got):
    vmem = pl.BlockSpec(memory_space=pltpu.VMEM)
    senders, both, columns = got.shape
    return pl.pallas_call(
        cut_kernel,
        out_shape=jax.ShapeDtypeStruct((senders * both // 2, columns), LOW),
        in_specs=[vmem],
        out_specs=vmem,
        compiler_params=pltpu.CompilerParams(vmem_limit_bytes=16 * 1024 * 1024),
    )(got)


def against(left, right):
    return lax.dot_general(left, right, (((0,), (0,)), ((), ())), preferred_element_type=F32)


def own_kernel(got_ref, mine_ref):
    half, columns = mine_ref.shape
    left = got_ref[:, :half, :].reshape(-1, columns)
    right = got_ref[:, half:, :].reshape(-1, columns)
    mine_ref[...] = against(left, right)


def own(got):
    vmem = pl.BlockSpec(memory_space=pltpu.VMEM)
    _, both, columns = got.shape
    return pl.pallas_call(
        own_kernel,
        out_shape=jax.ShapeDtypeStruct((both // 2, columns), F32),
        in_specs=[vmem],
        out_specs=vmem,
        compiler_params=pltpu.CompilerParams(vmem_limit_bytes=16 * 1024 * 1024),
        cost_estimate=pl.CostEstimate(flops=2**28, bytes_accessed=2**21, transcendentals=0),
    )(got)


def join_kernel(got_ref, other_ref, mine_ref, tile_ref):
    core = lax.axis_index("core")
    half = mine_ref.shape[0]
    _, depth, rows, columns = tile_ref.shape
    left = got_ref[:, :half, :].reshape(-1, columns)
    tile_ref[core] = mine_ref[...].reshape(depth, rows, columns)
    tile_ref[1 - core] = against(left, other_ref[...]).reshape(depth, rows, columns)


def join(got, other, mine, depth):
    vmem = pl.BlockSpec(memory_space=pltpu.VMEM)
    rows, columns = mine.shape
    return pl.pallas_call(
        join_kernel,
        out_shape=jax.ShapeDtypeStruct((2, depth // 2, rows * 2 // depth, columns), F32),
        in_specs=[vmem, vmem, vmem],
        out_specs=vmem,
        compiler_params=pltpu.CompilerParams(vmem_limit_bytes=16 * 1024 * 1024),
    )(got, other, mine)


def per_device(acts, up_grad):
    tokens, width = acts.shape
    owners = 64
    rows = width // owners
    plane = 8
    depth = 8
    core = lax.axis_index("core")
    halves = [
        lax.dynamic_slice_in_dim(acts, row * 512 + core * 256, 256, 1) for row in range(2)
    ]
    sent = jnp.stack(
        [
            jnp.concatenate([halves[i // 4], up_grad[:, i % 4 * 256 : i % 4 * 256 + 256]], axis=0)
            for i in range(plane)
        ]
    )
    got = lax.all_to_all(sent, PLANE, 0, 0, tiled=True)
    swap = [(0, 1), (1, 0)]
    other = lax.ppermute(cut(got), "core", swap)
    tile = join(got, other, own(got), depth)
    parts = lax.all_to_all(tile.reshape(depth, 64, 256), DEPTH, 0, 0, tiled=True)
    piece = (jnp.sum(parts, axis=0) / (tokens * owners)).astype(LOW)
    pieces = jnp.broadcast_to(piece[None], (depth // 2, 64, 256))
    tile = lax.all_to_all(pieces, "zh", 0, 0, tiled=True).reshape(256, 256)
    mine = lax.all_to_all(
        jnp.broadcast_to(tile[None], (plane, 256, 256)), PLANE, 0, 0, tiled=True
    )
    other = lax.ppermute(mine, "core", swap)
    found, total = roots(mine, other, rows, 128)
    found = lax.ppermute(found, ("zl", "core"), [(0, 0), (1, 2), (2, 1), (3, 3)])
    totals = lax.all_to_all(total, SPREAD, 0, 0, tiled=True)
    mean = jnp.sum(totals, axis=0, keepdims=True)[:, :1] / (width * width * 8)
    update = found[2 * rows :] * lax.rsqrt(mean + 1e-06)
    return (found[:rows], found[rows : 2 * rows], update)


def solution(mesh):
    fine = Mesh(mesh.devices.reshape(SIZES), NAMES)
    out = P(DP, TENSOR)
    return jax.shard_map(
        per_device,
        mesh=fine,
        in_specs=(P(DP, None), P(DP, TENSOR)),
        out_specs=(out, out, out),
        check_vma=False,
    )
```
